256 devices in a mesh: gz: 2 (over core), row: 4 (over x), col: 32 (over z, y).
Axes of the slice: x: 4, y: 4, z: 8, core: 2. Of those that a mesh axis runs over, the one named last changes fastest.
Arguments:
- right_sides: float32 [256, 4, 16, 256], P(('gz', 'row', 'col')), may hold values from -6 to 6
- lower_inverse: bfloat16 [256, 4, 256, 256], P(('gz', 'row', 'col')), may hold values from -0.375 to 0.375
- upper_inverse: bfloat16 [256, 4, 256, 256], P(('gz', 'row', 'col')), may hold values from -0.375 to 0.375
- lower_blocks: bfloat16 [256, 4, 2, 256, 256], P(('gz', 'row', 'col')), may hold values from -0.125 to 0.125
- upper_blocks: bfloat16 [256, 4, 2, 256, 256], P(('gz', 'row', 'col')), may hold values from -0.125 to 0.125
- node_widths: int32 [256, 4], P(('gz', 'row', 'col')), may hold values from 128 to 256, as said below
- far_levels: int32 [256, 4], P(('gz', 'row', 'col')), may hold values from 0 to 8, as said below
- owner_level: int32 [256], replicated, may hold values from 0 to 8, as said below
Outputs:
- solution: float32 [256, 4, 16, 256], P(('gz', 'row', 'col'))
The draws below stay inside these ranges and needn't reach their ends.
Inputs may be any that keep to these rules, and one draw needn't show every extreme that they name: Columns c >= node_widths of a supernode are padding; every device holds a supernode with all 256 columns. `far_levels`: between 2 and 8 where the supernode has two or more ancestors, but never past the root; 1 where it has one; 0 for the root and for the slot of the device that owns no separator. `owner_level`: every separator of level u is owned by exactly one device of its group (the devices t with the same t // 2**u); one device owns none and holds 0.
All inputs are finite; a program needn't handle non-finite values.
Results may differ from the reference program's by a relative error of at most 0.018.
Values may be sent and summed in bfloat16 or wider, within the bound.
No kernel may reach another device: no remote copies, remote signals or barrier semaphores. Data moves between devices by JAX's collectives and lax.ppermute only.
A program may use at most 64 MiB of HBM per device.

```python
import jax
import jax.numpy as jnp

W = 256
RHS = 16
NB = 2
LOCAL_LEVELS = 2
LOCAL_COUNT = 3
NODES = 4
SUBTREES = 256
UPPER = 8
REACH = 8


def owner_table(key):
    free_ids = jnp.arange(SUBTREES, dtype=jnp.int32)
    owned = jnp.zeros((SUBTREES,), jnp.int32)
    count = SUBTREES
    level = 0
    while count > 1:
        level = level + 1
        pairs = free_ids.reshape(count // 2, 2)
        coin = jax.random.randint(jax.random.fold_in(key, 100 + level), (count // 2,), 0, 2)
        chosen = jnp.where(coin == 1, pairs[:, 1], pairs[:, 0])
        staying = jnp.where(coin == 1, pairs[:, 0], pairs[:, 1])
        owned = owned.at[chosen].set(level)
        free_ids = staying
        count = count // 2
    return owned.astype(jnp.int32)


def draw_owner_level(key, part):
    return owner_table(key)


def draw_node_widths(key, part):
    key_one, key_two = jax.random.split(jax.random.fold_in(key, 23))
    widths = jax.random.randint(key_one, (SUBTREES, NODES), W // 2, W + 1)
    full_slot = jax.random.randint(key_two, (SUBTREES, 1), 0, NODES)
    slots = jnp.arange(NODES, dtype=jnp.int32)[None, :]
    return jnp.where(slots == full_slot, W, widths).astype(jnp.int32)


def draw_far_levels(key, part):
    owners = owner_table(key)
    identities = jnp.arange(SUBTREES, dtype=jnp.int32)
    slots = jnp.arange(NODES, dtype=jnp.int32)
    heights = jnp.zeros((NODES,), jnp.int32)
    for step_at in range(LOCAL_LEVELS):
        heights = jnp.where(slots >= 2 ** LOCAL_LEVELS - 2 ** (LOCAL_LEVELS - step_at), step_at, heights)
    local_room = LOCAL_LEVELS - 1 - heights + UPPER
    owned_room = jnp.where(owners > 0, UPPER - owners, 0)
    room_up = jnp.where(slots[None, :] == NODES - 1, owned_room[:, None], local_room[None, :])
    top_reach = jnp.minimum(room_up, REACH)
    random_bits = jax.random.randint(jax.random.fold_in(key, 31), (SUBTREES, NODES), 0, 1 << 20)
    picked = 2 + random_bits % jnp.maximum(top_reach - 1, 1)
    result = jnp.where(room_up >= 2, picked, room_up).astype(jnp.int32)
    group_owner = []
    for level in range(2, UPPER + 1):
        marked = jnp.where(owners == level, identities, 0)
        summed = marked.reshape(SUBTREES // 2 ** level, 2 ** level).sum(axis=1)
        group_owner.append(jnp.repeat(summed, 2 ** level))
    designated = jnp.zeros((SUBTREES,), jnp.int32)
    for index, level in enumerate(range(2, UPPER + 1)):
        holder = group_owner[index]
        beside = (identities == holder + 1) | (identities == holder - 1)
        designated = jnp.where(beside, level, designated)
    for index, level in enumerate(range(2, UPPER + 1)):
        holder = group_owner[index]
        across = identities == jnp.bitwise_xor(holder, 2 ** (level - 1))
        designated = jnp.where(across, level, designated)
    root_slot = (slots == LOCAL_COUNT - 1)[None, :]
    forced = root_slot & (designated[:, None] > 0)
    return jnp.where(forced, designated[:, None], result).astype(jnp.int32)


def steps_of(key, dims, cuts, smallest, high):
    def one(position, blocks):
        steps = jax.random.uniform(jax.random.fold_in(jax.random.fold_in(key, 6), position), (blocks,), jnp.float32, smallest / len(cuts), high / len(cuts))
        return jnp.repeat(jnp.exp(steps), dims[position] // blocks).reshape((-1,) + (1,) * (len(dims) - position - 1))

    factor_of = one(*cuts[0])
    for cut in cuts[1:]:
        factor_of = factor_of * one(*cut)
    return factor_of


def scatter_about(stream_key, dims, spread, bound, shards=(), kind=jnp.bfloat16):
    loudness = steps_of(stream_key, dims, shards, -0.22, 0.18) if shards else 1.0
    drawn = jax.random.normal(stream_key, dims, jnp.float32) * spread * loudness
    return jnp.minimum(jnp.maximum(drawn, -bound), bound).astype(kind)


def setup_inputs(seed: int = 0) -> dict:
    keys = jax.random.split(jax.random.key(seed), 9)
    return {
        "right_sides": scatter_about(keys[0], (SUBTREES, NODES, RHS, W), 1.0, 6.0, ((0, 256),), jnp.float32),
        "lower_inverse": scatter_about(keys[1], (SUBTREES, NODES, W, W), W ** -0.5, 0.375, ((0, 256),)),
        "upper_inverse": scatter_about(keys[2], (SUBTREES, NODES, W, W), W ** -0.5, 0.375, ((0, 256),)),
        "lower_blocks": scatter_about(keys[3], (SUBTREES, NODES, NB, W, W), (8 * W) ** -0.5, 0.125, ((0, 256),)),
        "upper_blocks": scatter_about(keys[4], (SUBTREES, NODES, NB, W, W), (8 * W) ** -0.5, 0.125, ((0, 256),)),
        "node_widths": draw_node_widths(jax.random.fold_in(keys[8], 71), 0),
        "far_levels": draw_far_levels(jax.random.fold_in(keys[8], 71), 0),
        "owner_level": draw_owner_level(jax.random.fold_in(keys[8], 71), 0),
    }


def level_start(height):
    return 2 ** LOCAL_LEVELS - 2 ** (LOCAL_LEVELS - height)


def apply_blocks(vectors, blocks):
    return jnp.einsum("snrk,snak->snra", vectors.astype(jnp.float32), blocks.astype(jnp.float32))


def apply_single(vectors, blocks):
    return jnp.einsum("srk,sak->sra", vectors.astype(jnp.float32), blocks.astype(jnp.float32))


def forward_local(right_sides, lower_inverse, lower_blocks, padding, far_levels, upper_levels):
    batch_size = right_sides.shape[0]
    pending = jnp.zeros((batch_size, LOCAL_COUNT, RHS, W), jnp.float32)
    upper_pending = jnp.zeros((batch_size, upper_levels, RHS, W), jnp.float32)
    solved = []
    for height in range(LOCAL_LEVELS):
        offset = level_start(height)
        amount = 2 ** (LOCAL_LEVELS - 1 - height)
        residue = (right_sides[:, offset:offset + amount] - pending[:, offset:offset + amount]).astype(jnp.bfloat16)
        solved_now = padding[:, offset:offset + amount] * apply_blocks(residue, lower_inverse[:, offset:offset + amount])
        solved.append(solved_now)
        rounded = solved_now.astype(jnp.bfloat16)
        for block_id in range(NB):
            product = apply_blocks(rounded, lower_blocks[:, offset:offset + amount, block_id])
            for distance in range(1, REACH + 1):
                if block_id == 0 and distance > 1:
                    continue
                if block_id == 0:
                    chosen = product
                else:
                    matches = far_levels[:, offset:offset + amount] == distance
                    chosen = jnp.where(matches[:, :, None, None], product, 0.0)
                target = height + distance
                if target < LOCAL_LEVELS:
                    target_count = amount // 2 ** distance
                    folded = chosen.reshape(batch_size, target_count, 2 ** distance, RHS, W).sum(axis=2)
                    begin_at = level_start(target)
                    pending = pending.at[:, begin_at:begin_at + target_count].add(folded)
                elif target - LOCAL_LEVELS < upper_levels:
                    upper_pending = upper_pending.at[:, target - LOCAL_LEVELS].add(chosen.sum(axis=1))
    return jnp.concatenate(solved, axis=1), upper_pending


def backward_local(forward, upper_inverse, upper_blocks, padding, far_levels, upper_known):
    upper_levels = upper_known.shape[1]
    solutions = [None] * LOCAL_LEVELS
    for height in reversed(range(LOCAL_LEVELS)):
        offset = level_start(height)
        amount = 2 ** (LOCAL_LEVELS - 1 - height)
        residue = forward[:, offset:offset + amount]
        for block_id in range(NB):
            operand = jnp.zeros(residue.shape, jnp.float32)
            for distance in range(1, REACH + 1):
                if block_id == 0 and distance > 1:
                    continue
                target = height + distance
                if target < LOCAL_LEVELS:
                    known_part = jnp.repeat(solutions[target], 2 ** distance, axis=1)
                elif target - LOCAL_LEVELS < upper_levels:
                    known_part = jnp.broadcast_to(upper_known[:, target - LOCAL_LEVELS][:, None], residue.shape)
                else:
                    continue
                if block_id == 0:
                    operand = known_part
                else:
                    matches = far_levels[:, offset:offset + amount] == distance
                    operand = operand + jnp.where(matches[:, :, None, None], known_part, 0.0)
            residue = residue - apply_blocks(operand.astype(jnp.bfloat16), upper_blocks[:, offset:offset + amount, block_id])
        solutions[height] = padding[:, offset:offset + amount] * apply_blocks(residue.astype(jnp.bfloat16), upper_inverse[:, offset:offset + amount])
    return jnp.concatenate(solutions, axis=1)


def reference(right_sides, lower_inverse, upper_inverse, lower_blocks, upper_blocks, node_widths, far_levels, owner_level):
    upper_levels = UPPER
    columns = jnp.arange(W, dtype=jnp.int32)
    padding = (columns[None, None, None, :] < node_widths[:, :, None, None]).astype(jnp.float32)
    forward_nodes, upper_pending = forward_local(
        right_sides[:, :LOCAL_COUNT], lower_inverse[:, :LOCAL_COUNT], lower_blocks[:, :LOCAL_COUNT],
        padding[:, :LOCAL_COUNT], far_levels[:, :LOCAL_COUNT], upper_levels)
    own_rights = right_sides[:, LOCAL_COUNT]
    own_padding = padding[:, LOCAL_COUNT]
    own_far = far_levels[:, LOCAL_COUNT]
    own_forward = jnp.zeros((SUBTREES, RHS, W), jnp.float32)
    for height in range(1, upper_levels + 1):
        group_size = 2 ** height
        totals = upper_pending[:, height - 1].reshape(SUBTREES // group_size, group_size, RHS, W).sum(axis=1)
        gathered = jnp.repeat(totals, group_size, axis=0)
        owner_here = (owner_level == height)[:, None, None]
        residue = (own_rights - gathered).astype(jnp.bfloat16)
        solved_now = jnp.where(owner_here, own_padding * apply_single(residue, lower_inverse[:, LOCAL_COUNT]), 0.0)
        own_forward = own_forward + solved_now
        rounded = solved_now.astype(jnp.bfloat16)
        for block_id in range(NB):
            product = apply_single(rounded, lower_blocks[:, LOCAL_COUNT, block_id])
            for distance in range(1, REACH + 1):
                if block_id == 0 and distance > 1:
                    continue
                target = height + distance
                if target > upper_levels:
                    continue
                if block_id == 0:
                    chosen = product
                else:
                    chosen = jnp.where((own_far == distance)[:, None, None], product, 0.0)
                upper_pending = upper_pending.at[:, target - 1].add(chosen)
    upper_known = jnp.zeros((SUBTREES, upper_levels, RHS, W), jnp.float32)
    own_solution = jnp.zeros((SUBTREES, RHS, W), jnp.float32)
    for height in range(upper_levels, 0, -1):
        group_size = 2 ** height
        owner_here = (owner_level == height)[:, None, None]
        residue = own_forward
        for block_id in range(NB):
            operand = jnp.zeros((SUBTREES, RHS, W), jnp.float32)
            for distance in range(1, REACH + 1):
                if block_id == 0 and distance > 1:
                    continue
                target = height + distance
                if target > upper_levels:
                    continue
                known_part = upper_known[:, target - 1]
                if block_id == 0:
                    operand = known_part
                else:
                    operand = operand + jnp.where((own_far == distance)[:, None, None], known_part, 0.0)
            residue = residue - apply_single(operand.astype(jnp.bfloat16), upper_blocks[:, LOCAL_COUNT, block_id])
        solved_now = jnp.where(owner_here, own_padding * apply_single(residue.astype(jnp.bfloat16), upper_inverse[:, LOCAL_COUNT]), 0.0)
        own_solution = own_solution + solved_now
        totals = solved_now.reshape(SUBTREES // group_size, group_size, RHS, W).sum(axis=1)
        upper_known = upper_known.at[:, height - 1].set(jnp.repeat(totals, group_size, axis=0))
    local_solution = backward_local(
        forward_nodes, upper_inverse[:, :LOCAL_COUNT], upper_blocks[:, :LOCAL_COUNT],
        padding[:, :LOCAL_COUNT], far_levels[:, :LOCAL_COUNT], upper_known)
    return jnp.concatenate([local_solution, own_solution[:, None]], axis=1)
```

```python
import functools

import jax
import jax.numpy as jnp
from jax import lax
from jax.experimental import pallas as pl
from jax.experimental.pallas import tpu as pltpu
from jax.sharding import Mesh
from jax.sharding import PartitionSpec as P

W = 256
RHS = 16
LOCAL_COUNT = 3
UPPER = 8
LOW = 2
DEVICES = 256
AXES = ("gz", "row", "col")
BF16 = jnp.bfloat16
F32 = jnp.float32
META = 16
VMEM = pl.BlockSpec(memory_space=pltpu.VMEM)
SMEM = pl.BlockSpec(memory_space=pltpu.SMEM)
PARAMS = pltpu.CompilerParams(vmem_limit_bytes=32 * 1024 * 1024)


def in_column(t):
    return (t % 4) == (0 if t < DEVICES // 2 else 2)


def partner(t, level):
    other = t ^ (1 << (level - 1))
    return other ^ 2 if level == UPPER else other


def exchange(value, level):
    pairs = [
        (t, partner(t, level)) for t in range(DEVICES) if level <= LOW or in_column(t)
    ]
    return lax.ppermute(value, AXES, pairs)


def over_y(value):
    total = None
    for step in (1, 2, 3):
        pairs = [
            (t, t - t % 4 + (t % 4 + step) % 4) for t in range(DEVICES) if in_column(t)
        ]
        came = lax.ppermute(value, AXES, pairs)
        total = came if total is None else total + came
    return total


def times(vectors, blocks):
    return jnp.dot(vectors, blocks, preferred_element_type=F32)


def times_rows(vectors, blocks):
    return lax.dot_general(
        vectors, blocks, (((1,), (1,)), ((), ())), preferred_element_type=F32
    )


def column_pad(width):
    return lax.broadcasted_iota(jnp.int32, (W, 1), 0) < width


def row_pad(width):
    return lax.broadcasted_iota(jnp.int32, (1, W), 1) < width


def combine_kernel(widths, far, linv, uinv, lblk, ublk, low, up):
    pad = column_pad(widths[0, LOCAL_COUNT])
    distance = jnp.full((META, W), far[0, LOCAL_COUNT], jnp.int32).astype(F32).astype(BF16)
    lower = jnp.where(pad, linv[0, 0], 0)
    upper = jnp.where(pad, uinv[0, 0], 0)
    for block in range(2):
        low[block * W : (block + 1) * W] = times(lblk[0, 0, block], lower).T.astype(BF16)
        up[block * W : (block + 1) * W] = times(upper, ublk[0, 0, block]).T.astype(BF16)
    up[2 * W : 3 * W] = times(upper, lower).T.astype(BF16)
    low[2 * W :] = distance
    up[3 * W :] = distance


def combine(widths, far, linv, uinv, lblk, ublk):
    slot = pl.BlockSpec((1, 1, W, W), lambda i: (0, LOCAL_COUNT, 0, 0))
    pair = pl.BlockSpec((1, 1, 2, W, W), lambda i: (0, LOCAL_COUNT, 0, 0, 0))
    return pl.pallas_call(
        combine_kernel,
        grid=(1,),
        in_specs=[SMEM, SMEM, slot, slot, pair, pair],
        out_specs=[
            pl.BlockSpec((2 * W + META, W), lambda i: (0, 0)),
            pl.BlockSpec((3 * W + META, W), lambda i: (0, 0)),
        ],
        out_shape=[
            jax.ShapeDtypeStruct((2 * W + META, W), BF16),
            jax.ShapeDtypeStruct((3 * W + META, W), BF16),
        ],
        compiler_params=PARAMS,
    )(widths, far, linv, uinv, lblk, ublk)


def leaves_kernel(widths, far, level, rights, linv, lblk, solved, sums, halves):
    own = rights[0, LOCAL_COUNT]
    for v in range(1, UPPER + 1):
        sums[(v - 1) * RHS : v * RHS] = jnp.where(level[0] == v, own, 0.0)
    pending = jnp.zeros((RHS, W), F32)
    for slot in range(LOCAL_COUNT):
        residue = rights[0, slot]
        if slot == LOCAL_COUNT - 1:
            residue = residue - pending
        forward = jnp.where(
            row_pad(widths[0, slot]), times_rows(residue.astype(BF16), linv[0, slot]), 0.0
        )
        solved[slot] = forward
        half = forward.astype(BF16)
        near = times_rows(half, lblk[0, slot, 0])
        away = times_rows(half, lblk[0, slot, 1])
        if slot == LOCAL_COUNT - 1:
            sums[:RHS] = sums[:RHS] - near
            target = far[0, slot]
        else:
            pending = pending + near
            target = far[0, slot] - 1
        for v in range(1, UPPER + 1):
            rows = slice((v - 1) * RHS, v * RHS)
            sums[rows] = sums[rows] - jnp.where(target == v, away, 0.0)
    halves[...] = sums[...].astype(BF16)


def leaves(widths, far, level, rights, linv, lblk):
    return pl.pallas_call(
        leaves_kernel,
        grid=(1,),
        in_specs=[
            SMEM,
            SMEM,
            SMEM,
            pl.BlockSpec((1, 4, RHS, W), lambda i: (0, 0, 0, 0)),
            pl.BlockSpec((1, LOCAL_COUNT, W, W), lambda i: (0, 0, 0, 0)),
            pl.BlockSpec((1, LOCAL_COUNT, 2, W, W), lambda i: (0, 0, 0, 0, 0)),
        ],
        out_specs=[
            pl.BlockSpec((LOCAL_COUNT, RHS, W), lambda i: (0, 0, 0)),
            pl.BlockSpec((UPPER * RHS, W), lambda i: (0, 0)),
            pl.BlockSpec((UPPER * RHS, W), lambda i: (0, 0)),
        ],
        out_shape=[
            jax.ShapeDtypeStruct((LOCAL_COUNT, RHS, W), F32),
            jax.ShapeDtypeStruct((UPPER * RHS, W), F32),
            jax.ShapeDtypeStruct((UPPER * RHS, W), BF16),
        ],
        compiler_params=PARAMS,
    )(widths, far, level, rights, linv, lblk)


def climb_kernel(count, sums, came, low, residue, rest, halves):
    total = sums[...] + came[...].astype(F32)
    half = total[:RHS].astype(BF16)
    residue[...] = half
    near = times(half, low[:W])
    away = times(half, low[W : 2 * W])
    distance = low[2 * W : 2 * W + 1].astype(F32)
    for step in range(1, count):
        value = total[step * RHS : (step + 1) * RHS]
        if step == 1:
            value = value - near
        value = value - jnp.where(distance == float(step), away, 0.0)
        rest[(step - 1) * RHS : step * RHS] = value
        halves[(step - 1) * RHS : step * RHS] = value.astype(BF16)


def climb(sums, came, low):
    count = sums.shape[0] // RHS
    rows = (count - 1) * RHS
    return pl.pallas_call(
        functools.partial(climb_kernel, count),
        in_specs=[VMEM] * 3,
        out_specs=[VMEM] * 3,
        out_shape=[
            jax.ShapeDtypeStruct((RHS, W), BF16),
            jax.ShapeDtypeStruct((rows, W), F32),
            jax.ShapeDtypeStruct((rows, W), BF16),
        ],
        compiler_params=PARAMS,
    )(sums, came, low)


def separator(residue, up, above):
    value = times(residue, up[2 * W : 3 * W])
    if not above:
        return value
    distance = up[3 * W : 3 * W + 1].astype(F32)
    known = jnp.zeros((RHS, W), F32)
    for step, part in enumerate(above, 1):
        known = known + jnp.where(distance == float(step), part.astype(F32), 0.0)
    return value - times(above[0], up[:W]) - times(known.astype(BF16), up[W : 2 * W])


def top_kernel(*refs):
    amount = UPPER - LOW
    residues, ups, out = (refs[:amount], refs[amount : 2 * amount], refs[2 * amount])
    above = []
    for v in range(UPPER, LOW, -1):
        value = separator(residues[v - LOW - 1][...], ups[v - LOW - 1], above).astype(BF16)
        out[(v - LOW - 1) * RHS : (v - LOW) * RHS] = value
        above = [value] + above


def top(residues, ups):
    return pl.pallas_call(
        top_kernel,
        in_specs=[VMEM] * (2 * (UPPER - LOW)),
        out_specs=VMEM,
        out_shape=jax.ShapeDtypeStruct(((UPPER - LOW) * RHS, W), BF16),
        compiler_params=PARAMS,
    )(*residues, *ups)


def descend_kernel(widths, far, level, solved, known, r1, r2, u1, u2, uinv, ublk, out):
    above = [known[k * RHS : (k + 1) * RHS] for k in range(UPPER - LOW)]
    own = jnp.zeros((RHS, W), F32)
    for k, part in enumerate(above):
        own = jnp.where(level[0] == k + LOW + 1, part.astype(F32), own)
    for v, residue, up in ((2, r2, u2), (1, r1, u1)):
        value = separator(residue[...], up, above)
        own = jnp.where(level[0] == v, value, own)
        above = [value.astype(BF16)] + above
    out[0, LOCAL_COUNT] = own
    for slot in (2, 1, 0):
        distant = jnp.zeros((RHS, W), F32)
        for step, part in enumerate(above, 1):
            distant = distant + jnp.where(far[0, slot] == step, part.astype(F32), 0.0)
        residue = (
            solved[slot]
            - times_rows(above[0], ublk[0, slot, 0])
            - times_rows(distant.astype(BF16), ublk[0, slot, 1])
        )
        value = jnp.where(
            row_pad(widths[0, slot]), times_rows(residue.astype(BF16), uinv[0, slot]), 0.0
        )
        out[0, slot] = value
        if slot == 2:
            above = [value.astype(BF16)] + above


def descend(widths, far, level, solved, known, r1, r2, u1, u2, uinv, ublk):
    def whole(array):
        return pl.BlockSpec(array.shape, lambda i: (0,) * array.ndim)

    return pl.pallas_call(
        descend_kernel,
        grid=(1,),
        in_specs=[
            SMEM,
            SMEM,
            SMEM,
            whole(solved),
            whole(known),
            whole(r1),
            whole(r2),
            whole(u1),
            whole(u2),
            pl.BlockSpec((1, LOCAL_COUNT, W, W), lambda i: (0, 0, 0, 0)),
            pl.BlockSpec((1, LOCAL_COUNT, 2, W, W), lambda i: (0, 0, 0, 0, 0)),
        ],
        out_specs=pl.BlockSpec((1, 4, RHS, W), lambda i: (0, 0, 0, 0)),
        out_shape=jax.ShapeDtypeStruct((1, 4, RHS, W), F32),
        compiler_params=PARAMS,
    )(widths, far, level, solved, known, r1, r2, u1, u2, uinv, ublk)


def local(rights, linv, uinv, lblk, ublk, widths, far, owner_level):
    device = (
        lax.axis_index("gz") * lax.axis_size("row") + lax.axis_index("row")
    ) * lax.axis_size("col") + lax.axis_index("col")
    everyone = jnp.arange(DEVICES, dtype=jnp.int32)
    level = jnp.sum(jnp.where(everyone == device, owner_level, 0)).reshape(1)
    heights = jnp.arange(1, UPPER + 1, dtype=jnp.int32)[:, None]
    same_half = (everyone[None, :] >> (heights - 1)) == (device >> (heights - 1))
    here = jnp.any(same_half & (owner_level[None, :] == heights), axis=1)
    low, up = combine(widths, far, linv, uinv, lblk, ublk)
    solved, sums, halves = leaves(widths, far, level, rights, linv, lblk)
    residues = []
    ups = []
    for v in range(1, UPPER + 1):
        mine = here[v - 1]
        came = exchange(halves, v)
        if v < UPPER:
            low_came = exchange(low, v)
            low_here = jnp.where(mine, low, low_came)
            low = jnp.where(mine, low_came, low)
        up_came = exchange(up, v)
        ups.append(jnp.where(mine, up, up_came))
        up = jnp.where(mine, up_came, up)
        if v < UPPER:
            residue, sums, halves = climb(sums, came, low_here)
        else:
            residue = (sums + came.astype(F32)).astype(BF16)
        residues.append(residue)
    known = top(residues[LOW:], ups[LOW:])
    shared = over_y(known)
    y = device % 4
    column = jnp.where(device < DEVICES // 2, y == 0, y == 2)
    known = jnp.where(column, known, shared)
    return descend(
        widths, far, level, solved, known, residues[0], residues[1], ups[0], ups[1], uinv, ublk
    )


def solution(mesh):
    split = P(AXES)
    in_specs = (split,) * 7 + (P(),)
    return jax.shard_map(local, mesh=mesh, in_specs=in_specs, out_specs=split, check_vma=False)
```

```python
import functools

import jax
import jax.numpy as jnp
from jax import lax
from jax.experimental import pallas as pl
from jax.experimental.pallas import tpu as pltpu
from jax.sharding import PartitionSpec as P

W = 256
RHS = 16
LOCAL_COUNT = 3
UPPER = 8
LOW = 2
DEVICES = 256
AXES = ("gz", "row", "col")
BF16 = jnp.bfloat16
F32 = jnp.float32
FAR_A = 2 * W
SUMS = 2 * W + RHS
FAR_B = 3 * W
ROWS = 3 * W + RHS
OTHER_PAIR = UPPER
ROLE_A = UPPER + 1
FLAGS = UPPER + 2
VMEM = pl.BlockSpec(memory_space=pltpu.VMEM)
HBM = pl.BlockSpec(memory_space=pltpu.HBM)
PARAMS = pltpu.CompilerParams(vmem_limit_bytes=24 * 1024 * 1024)


def seat(t):
    return (t % 4 - (0 if t < DEVICES // 2 else 2)) % 4


def at_seat(t, place):
    return t - t % 4 + (place + (0 if t < DEVICES // 2 else 2)) % 4


def send(value, pairs):
    return lax.ppermute(value, AXES, pairs)


def seats(moves):
    firsts = [t for t in range(DEVICES) if t % 4 == 0]
    return [(at_seat(t, a), at_seat(t, b)) for t in firsts for a, b in moves]


def across(level):
    return [(t, t ^ (1 << (level - 1))) for t in range(DEVICES) if seat(t) < 2]


def layers(a, b):
    firsts = [t for t in range(DEVICES) if t % 4 == 0]
    return [(at_seat(t, a), at_seat(t ^ (DEVICES // 2), b)) for t in firsts]


def times(vectors, blocks):
    return jnp.dot(vectors, blocks, preferred_element_type=F32)


def times_rows(vectors, blocks):
    return lax.dot_general(
        vectors, blocks, (((1,), (1,)), ((), ())), preferred_element_type=F32
    )


def row_pad(width):
    return lax.broadcasted_iota(jnp.int32, (1, W), 1) < width


def part(rows, index):
    return rows[index * RHS : (index + 1) * RHS]


def begin_kernel(
    rights_in,
    linv_in,
    uinv_in,
    lblk_in,
    ublk_in,
    widths_in,
    far_in,
    owner,
    first,
    second,
    solved,
    sums,
    flags,
    level,
    rights,
    linv,
    uinv,
    lblk,
    ublk,
    widths,
    far,
    sems,
):
    own = pl.ds(LOCAL_COUNT, 1)
    rest = pl.ds(0, LOCAL_COUNT)
    small = [
        pltpu.make_async_copy(widths_in, widths, sems.at[0]),
        pltpu.make_async_copy(far_in, far, sems.at[1]),
    ]
    mine = [
        pltpu.make_async_copy(linv_in.at[0, own], linv.at[own], sems.at[2]),
        pltpu.make_async_copy(lblk_in.at[0, own], lblk.at[own], sems.at[3]),
        pltpu.make_async_copy(uinv_in.at[0, own], uinv, sems.at[4]),
        pltpu.make_async_copy(ublk_in.at[0, own], ublk, sems.at[5]),
    ]
    leaf = [
        pltpu.make_async_copy(rights_in.at[0], rights, sems.at[6]),
        pltpu.make_async_copy(linv_in.at[0, rest], linv.at[rest], sems.at[7]),
        pltpu.make_async_copy(lblk_in.at[0, rest], lblk.at[rest], sems.at[8]),
    ]
    for copy in small + mine + leaf:
        copy.start()
    gz = lax.axis_index("gz")
    col = lax.axis_index("col")
    me = gz * (DEVICES // 2) + lax.axis_index("row") * (DEVICES // 8) + col
    y = col % 4
    place = (y + 2 * gz) % 4
    everyone = lax.broadcasted_iota(jnp.int32, (1, DEVICES), 1)
    owners = owner[...]

    def spread(value):
        return jnp.broadcast_to(value, (RHS, W))

    def found(chosen):
        return spread(jnp.max(jnp.where(chosen, 1.0, 0.0), axis=1, keepdims=True))

    for v in range(1, UPPER + 1):
        half = lax.shift_right_logical(everyone, v - 1) == lax.shift_right_logical(me, v - 1)
        flags[(v - 1) * RHS : v * RHS] = found(half & (owners == v)).astype(BF16)
    flags[OTHER_PAIR * RHS : (OTHER_PAIR + 1) * RHS] = found(
        (everyone == (me ^ 2)) & (owners == 1)
    ).astype(BF16)
    flags[ROLE_A * RHS : (ROLE_A + 1) * RHS] = jnp.full(
        (RHS, W), jnp.where(place == 0, 1.0, 0.0), F32
    ).astype(BF16)
    my_level = spread(
        jnp.sum(jnp.where(everyone == me, owners, 0).astype(F32), axis=1, keepdims=True)
    )
    level[...] = my_level
    for copy in small + mine:
        copy.wait()
    pad = lax.broadcasted_iota(jnp.int32, (W, 1), 0) < widths[0, LOCAL_COUNT]
    distance = jnp.full((RHS, W), far[0, LOCAL_COUNT], jnp.int32).astype(F32).astype(BF16)
    lower = jnp.where(pad, linv[LOCAL_COUNT].astype(F32), 0.0).astype(BF16)
    upper = jnp.where(pad, uinv[0].astype(F32), 0.0).astype(BF16)
    low_blocks = [times(lblk[LOCAL_COUNT, b], lower).T.astype(BF16) for b in range(2)]
    up_blocks = [times(upper, ublk[0, b]).T.astype(BF16) for b in range(2)]
    up_blocks.append(times(upper, lower).T.astype(BF16))
    for copy in leaf:
        copy.wait()
    for v in range(1, UPPER + 1):
        sums[(v - 1) * RHS : v * RHS] = jnp.where(my_level == v, rights[LOCAL_COUNT], 0.0)
    pending = jnp.zeros((RHS, W), F32)
    for slot in range(LOCAL_COUNT):
        residue = rights[slot]
        if slot == LOCAL_COUNT - 1:
            residue = residue - pending
        forward = jnp.where(
            row_pad(widths[0, slot]), times_rows(residue.astype(BF16), linv[slot]), 0.0
        )
        solved[slot] = forward
        half = forward.astype(BF16)
        near = times_rows(half, lblk[slot, 0])
        away = times_rows(half, lblk[slot, 1])
        if slot == LOCAL_COUNT - 1:
            sums[:RHS] = sums[:RHS] - near
            target = far[0, slot]
        else:
            pending = pending + near
            target = far[0, slot] - 1
        for v in range(1, UPPER + 1):
            rows = slice((v - 1) * RHS, v * RHS)
            sums[rows] = sums[rows] - jnp.where(target == v, away, 0.0)
    halves = sums[...].astype(BF16)

    def write(low, up):
        for b in range(2):
            low[b * W : (b + 1) * W] = low_blocks[b]
        low[FAR_A : FAR_A + RHS] = distance
        low[SUMS : SUMS + UPPER * RHS] = halves
        low[SUMS + UPPER * RHS :] = jnp.zeros((ROWS - SUMS - UPPER * RHS, W), BF16)
        for b in range(3):
            up[b * W : (b + 1) * W] = up_blocks[b]
        up[FAR_B:] = distance

    @pl.when(place % 2 == 0)
    def _():
        write(first, second)

    @pl.when(place % 2 == 1)
    def _():
        write(second, first)


def begin(rights, linv, uinv, lblk, ublk, widths, far, owner):
    return pl.pallas_call(
        begin_kernel,
        in_specs=[HBM] * 7 + [VMEM],
        out_specs=[VMEM] * 6,
        out_shape=[
            jax.ShapeDtypeStruct((ROWS, W), BF16),
            jax.ShapeDtypeStruct((ROWS, W), BF16),
            jax.ShapeDtypeStruct((LOCAL_COUNT, RHS, W), F32),
            jax.ShapeDtypeStruct((UPPER * RHS, W), F32),
            jax.ShapeDtypeStruct((FLAGS * RHS, W), BF16),
            jax.ShapeDtypeStruct((RHS, W), F32),
        ],
        scratch_shapes=[
            pltpu.VMEM((4, RHS, W), F32),
            pltpu.VMEM((4, W, W), BF16),
            pltpu.VMEM((1, W, W), BF16),
            pltpu.VMEM((4, 2, W, W), BF16),
            pltpu.VMEM((1, 2, W, W), BF16),
            pltpu.SMEM((1, 4), jnp.int32),
            pltpu.SMEM((1, 4), jnp.int32),
            pltpu.SemaphoreType.DMA((9,)),
        ],
        compiler_params=PARAMS,
    )(rights, linv, uinv, lblk, ublk, widths, far, owner)


def flag(flags, index):
    return part(flags, index).astype(F32) > 0.5


def choose(test, one, other):
    return jnp.where(test, one.astype(F32), other.astype(F32)).astype(BF16)


def choose_rows(test, one, other, chosen, left):
    wide = jnp.concatenate([test] * 16, axis=0)
    for start in range(0, ROWS, W):
        rows = slice(start, min(start + W, ROWS))
        amount = rows.stop - rows.start
        a, b = (one[rows], other[rows])
        chosen[rows] = choose(wide[:amount], a, b)
        left[rows] = choose(wide[:amount], b, a)


def eliminate(total, low):
    half = total[:RHS].astype(BF16)
    near = times(half, low[:W])
    away = times(half, low[W : 2 * W])
    distance = low[FAR_A : FAR_A + RHS].astype(F32)
    rest = []
    for step in range(1, total.shape[0] // RHS):
        value = part(total, step)
        if step == 1:
            value = value - near
        rest.append(value - jnp.where(distance == float(step), away, 0.0))
    return half, jnp.concatenate(rest, axis=0)


def pass_on(flags, rest, left):
    rows = rest.shape[0]
    wide = jnp.concatenate([flag(flags, ROLE_A)] * (rows // RHS), axis=0)
    left[SUMS : SUMS + rows] = choose(wide, rest.astype(BF16), left[SUMS : SUMS + rows])


def climb_low_kernel(own, r1, r2, r3, sums, flags, k1, k1q, k2, left, residues, rest, lp, lq):
    choose_rows(flag(flags, 0), own, r1, k1, lp)
    choose_rows(flag(flags, OTHER_PAIR), r2, r3, k1q, lq)
    choose_rows(flag(flags, 1), lp, lq, k2, left)
    rows = slice(SUMS, SUMS + UPPER * RHS)
    near = sums[...] + r1[rows].astype(F32)
    other = r2[rows].astype(F32) + r3[rows].astype(F32)
    half, near = eliminate(near, k1)
    residues[:RHS] = half
    half, other = eliminate(other, k1q)
    residues[RHS : 2 * RHS] = half
    half, value = eliminate(near + other, k2)
    residues[2 * RHS :] = half
    rest[...] = value
    pass_on(flags, value, left)


def climb_low(own, r1, r2, r3, sums, flags):
    message = jax.ShapeDtypeStruct((ROWS, W), BF16)
    return pl.pallas_call(
        climb_low_kernel,
        in_specs=[VMEM] * 6,
        out_specs=[VMEM] * 6,
        out_shape=[
            message,
            message,
            message,
            message,
            jax.ShapeDtypeStruct((3 * RHS, W), BF16),
            jax.ShapeDtypeStruct(((UPPER - LOW) * RHS, W), F32),
        ],
        scratch_shapes=[pltpu.VMEM((ROWS, W), BF16)] * 2,
        compiler_params=PARAMS,
    )(own, r1, r2, r3, sums, flags)


def climb_kernel(height, own, came, sums, flags, chosen, left, residue, rest):
    choose_rows(flag(flags, height - 1), own, came, chosen, left)
    total = sums[...] + came[SUMS : SUMS + sums.shape[0]].astype(F32)
    half, value = eliminate(total, chosen)
    residue[...] = half
    rest[...] = value
    pass_on(flags, value, left)


def climb(height, own, came, sums, flags):
    message = jax.ShapeDtypeStruct((ROWS, W), BF16)
    return pl.pallas_call(
        functools.partial(climb_kernel, height),
        in_specs=[VMEM] * 4,
        out_specs=[VMEM] * 4,
        out_shape=[
            message,
            message,
            jax.ShapeDtypeStruct((RHS, W), BF16),
            jax.ShapeDtypeStruct((sums.shape[0] - RHS, W), F32),
        ],
        compiler_params=PARAMS,
    )(own, came, sums, flags)


def separator(residue, up, above):
    distance = up[FAR_B : FAR_B + RHS].astype(F32)
    known = jnp.zeros((RHS, W), F32)
    for step, value in enumerate(above, 1):
        known = known + jnp.where(distance == float(step), value.astype(F32), 0.0)
    return (
        times(residue, up[2 * W : 3 * W])
        - times(above[0], up[:W])
        - times(known.astype(BF16), up[W : 2 * W])
    ).astype(BF16)


def top_kernel(vectors, root, mine, came, flags, *refs):
    ups, (near_out, other_out) = (refs[:-2], refs[-2:])
    wide = jnp.concatenate([flag(flags, UPPER - 1)] * 16, axis=0)
    last = choose(wide, mine[2 * W : 3 * W], came[...])
    residue = part(vectors, UPPER).astype(F32) + root[...].astype(F32)
    above = [times(residue.astype(BF16), last).astype(BF16)]
    for v in range(UPPER - 1, LOW - 1, -1):
        above = [separator(part(vectors, v), ups[v], above)] + above
    for k, out in ((0, near_out), (1, other_out)):
        out[:RHS] = separator(part(vectors, k), ups[k], above)
        for step, value in enumerate(above, 1):
            out[step * RHS : (step + 1) * RHS] = value


def top(vectors, root, mine, came, flags, ups):
    known = jax.ShapeDtypeStruct((UPPER * RHS, W), BF16)
    return pl.pallas_call(
        top_kernel,
        in_specs=[VMEM] * (5 + len(ups)),
        out_specs=[VMEM] * 2,
        out_shape=[known, known],
        compiler_params=PARAMS,
    )(vectors, root, mine, came, flags, *ups)


def descend_kernel(
    uinv_in,
    ublk_in,
    widths_in,
    far_in,
    level,
    solved,
    own,
    a,
    b,
    c,
    out,
    uinv,
    ublk,
    widths,
    far,
    known,
    sems,
):
    rest = pl.ds(0, LOCAL_COUNT)
    copies = [
        pltpu.make_async_copy(widths_in, widths, sems.at[0]),
        pltpu.make_async_copy(far_in, far, sems.at[1]),
        pltpu.make_async_copy(uinv_in.at[0, rest], uinv, sems.at[2]),
        pltpu.make_async_copy(ublk_in.at[0, rest], ublk, sems.at[3]),
    ]
    for copy in copies:
        copy.start()
    place = (lax.axis_index("col") % 4 + 2 * lax.axis_index("gz")) % 4
    for seated, ref in ((0, a), (1, own), (2, b), (3, c)):

        @pl.when(place == seated)
        def _():
            known[...] = ref[...]

    above = [part(known, k) for k in range(UPPER)]
    own_value = jnp.zeros((RHS, W), F32)
    for k, value in enumerate(above):
        own_value = jnp.where(level[...] == k + 1, value.astype(F32), own_value)
    out[0, LOCAL_COUNT] = own_value
    for copy in copies:
        copy.wait()
    for slot in (2, 1, 0):
        distant = jnp.zeros((RHS, W), F32)
        for step, value in enumerate(above, 1):
            distant = distant + jnp.where(far[0, slot] == step, value.astype(F32), 0.0)
        residue = (
            solved[slot]
            - times_rows(above[0], ublk[slot, 0])
            - times_rows(distant.astype(BF16), ublk[slot, 1])
        )
        value = jnp.where(
            row_pad(widths[0, slot]), times_rows(residue.astype(BF16), uinv[slot]), 0.0
        )
        out[0, slot] = value
        if slot == 2:
            above = [value.astype(BF16)] + above


def descend(uinv, ublk, widths, far, level, solved, own, a, b, c):
    return pl.pallas_call(
        descend_kernel,
        in_specs=[HBM] * 4 + [VMEM] * 6,
        out_specs=VMEM,
        out_shape=jax.ShapeDtypeStruct((1, 4, RHS, W), F32),
        scratch_shapes=[
            pltpu.VMEM((LOCAL_COUNT, W, W), BF16),
            pltpu.VMEM((LOCAL_COUNT, 2, W, W), BF16),
            pltpu.SMEM((1, 4), jnp.int32),
            pltpu.SMEM((1, 4), jnp.int32),
            pltpu.VMEM((UPPER * RHS, W), BF16),
            pltpu.SemaphoreType.DMA((4,)),
        ],
        compiler_params=PARAMS,
    )(uinv, ublk, widths, far, level, solved, own, a, b, c)


def local(rights, linv, uinv, lblk, ublk, widths, far, owner_level):
    first, second, solved, sums, flags, level = begin(
        rights, linv, uinv, lblk, ublk, widths, far, owner_level.reshape(1, DEVICES)
    )
    r1 = send(second, seats(((1, 0), (0, 1))))
    r2 = send(first, seats(((2, 0), (3, 1))))
    r3 = send(second, seats(((3, 0), (2, 1))))
    near, other, above, message, residues, sums = climb_low(first, r1, r2, r3, sums, flags)
    ups = [near, other, above]
    vectors = [residues]
    for height in range(LOW + 1, UPPER):
        came = send(message, across(height))
        chosen, message, residue, sums = climb(height, message, came, sums, flags)
        ups.append(chosen)
        vectors.append(residue)
    root = sums.astype(BF16)
    root_came = send(root, layers(0, 1))
    vectors = send(jnp.concatenate(vectors + [root], axis=0), seats(((0, 1),)))
    last_came = send(message[2 * W : 3 * W], layers(1, 1))
    known, known_other = top(vectors, root_came, message, last_came, flags, ups)
    a = send(known, seats(((1, 0),)))
    b = send(known_other, seats(((1, 2),)))
    c = send(known_other, seats(((1, 3),)))
    return descend(uinv, ublk, widths, far, level, solved, known, a, b, c)


def solution(mesh):
    split = P(AXES)
    in_specs = (split,) * 7 + (P(),)
    return jax.shard_map(local, mesh=mesh, in_specs=in_specs, out_specs=split, check_vma=False)
```

```python
import functools

import jax
import jax.numpy as jnp
from jax import lax
from jax.experimental import pallas as pl
from jax.experimental.pallas import tpu as pltpu
from jax.sharding import PartitionSpec as P

W = 256
RHS = 16
LOCAL_COUNT = 3
UPPER = 8
LOW = 2
DEVICES = 256
AXES = ("gz", "row", "col")
BF16 = jnp.bfloat16
F32 = jnp.float32
FAR_A = 2 * W
SUMS = 2 * W + RHS
FAR_B = 3 * W
ROWS = 3 * W + RHS
GATHERS = (1, 3, 6)
OTHER_PAIR = {low: UPPER + k for k, low in enumerate(GATHERS)}
ROLE_A = UPPER + len(GATHERS)
FLAGS = ROLE_A + 1
LEADERS = (1, 6)
VMEM = pl.BlockSpec(memory_space=pltpu.VMEM)
HBM = pl.BlockSpec(memory_space=pltpu.HBM)
PARAMS = pltpu.CompilerParams(vmem_limit_bytes=24 * 1024 * 1024)
BEGIN_PARAMS = pltpu.CompilerParams(vmem_limit_bytes=60 * 1024 * 1024)


def seat(t):
    return (t % 4 - (0 if t < DEVICES // 2 else 2)) % 4


def at_seat(t, place):
    return t - t % 4 + (place + (0 if t < DEVICES // 2 else 2)) % 4


def send(value, pairs):
    return lax.ppermute(value, AXES, pairs)


def seats(moves):
    firsts = [t for t in range(DEVICES) if t % 4 == 0]
    return [(at_seat(t, a), at_seat(t, b)) for t in firsts for a, b in moves]


def leads(t):
    return seat(t) < 2 and t // 4 % 8 in LEADERS


def to_leaders(distance):
    return [(t ^ (4 * distance), t) for t in range(DEVICES) if leads(t)]


def from_leaders(distance):
    return [(t, t ^ (4 * distance)) for t in range(DEVICES) if leads(t) and seat(t) == 1]


def across(mask):
    return [(t, t ^ mask) for t in range(DEVICES) if leads(t)]


def layers(a, b):
    firsts = [t for t in range(DEVICES) if t % 4 == 0 and t // 4 % 8 in LEADERS]
    return [(at_seat(t, a), at_seat(t ^ (DEVICES // 2), b)) for t in firsts]


def times(vectors, blocks):
    return jnp.dot(vectors, blocks, preferred_element_type=F32)


def times_rows(vectors, blocks):
    return lax.dot_general(
        vectors, blocks, (((1,), (1,)), ((), ())), preferred_element_type=F32
    )


def row_pad(width):
    return lax.broadcasted_iota(jnp.int32, (1, W), 1) < width


def part(rows, index):
    return rows[index * RHS : (index + 1) * RHS]


def begin_kernel(
    rights_in,
    linv_in,
    uinv_in,
    lblk_in,
    ublk_in,
    widths_in,
    far_in,
    owner,
    first,
    second,
    solved,
    sums,
    flags,
    level,
    rights,
    linv,
    uinv,
    lblk,
    ublk,
    widths,
    far,
    sems,
):
    own = pl.ds(LOCAL_COUNT, 1)
    rest = pl.ds(0, LOCAL_COUNT)
    small = [
        pltpu.make_async_copy(widths_in, widths, sems.at[0]),
        pltpu.make_async_copy(far_in, far, sems.at[1]),
    ]
    mine = [
        pltpu.make_async_copy(linv_in.at[0, own], linv.at[own], sems.at[2]),
        pltpu.make_async_copy(lblk_in.at[0, own], lblk.at[own], sems.at[3]),
        pltpu.make_async_copy(uinv_in.at[0, own], uinv, sems.at[4]),
        pltpu.make_async_copy(ublk_in.at[0, own], ublk, sems.at[5]),
    ]
    leaf = [
        pltpu.make_async_copy(rights_in.at[0], rights, sems.at[6]),
        pltpu.make_async_copy(linv_in.at[0, rest], linv.at[rest], sems.at[7]),
        pltpu.make_async_copy(lblk_in.at[0, rest], lblk.at[rest], sems.at[8]),
    ]
    for copy in small + mine + leaf:
        copy.start()
    gz = lax.axis_index("gz")
    col = lax.axis_index("col")
    me = gz * (DEVICES // 2) + lax.axis_index("row") * (DEVICES // 8) + col
    y = col % 4
    place = (y + 2 * gz) % 4
    everyone = lax.broadcasted_iota(jnp.int32, (1, DEVICES), 1)
    owners = owner[...]

    def spread(value):
        return jnp.broadcast_to(value, (RHS, W))

    def found(chosen):
        return spread(jnp.max(jnp.where(chosen, 1.0, 0.0), axis=1, keepdims=True))

    for v in range(1, UPPER + 1):
        half = lax.shift_right_logical(everyone, v - 1) == lax.shift_right_logical(me, v - 1)
        flags[(v - 1) * RHS : v * RHS] = found(half & (owners == v)).astype(BF16)
    for v in GATHERS:
        half = lax.shift_right_logical(everyone, v - 1) == (
            lax.shift_right_logical(me, v - 1) ^ 2
        )
        flags[OTHER_PAIR[v] * RHS : (OTHER_PAIR[v] + 1) * RHS] = found(
            half & (owners == v)
        ).astype(BF16)
    flags[ROLE_A * RHS : (ROLE_A + 1) * RHS] = jnp.full(
        (RHS, W), jnp.where(place == 0, 1.0, 0.0), F32
    ).astype(BF16)
    my_level = spread(
        jnp.sum(jnp.where(everyone == me, owners, 0).astype(F32), axis=1, keepdims=True)
    )
    level[...] = my_level
    for copy in small + mine:
        copy.wait()
    pad = lax.broadcasted_iota(jnp.int32, (W, 1), 0) < widths[0, LOCAL_COUNT]
    distance = jnp.full((RHS, W), far[0, LOCAL_COUNT], jnp.int32).astype(F32).astype(BF16)
    lower = jnp.where(pad, linv[LOCAL_COUNT].astype(F32), 0.0).astype(BF16)
    upper = jnp.where(pad, uinv[0].astype(F32), 0.0).astype(BF16)
    low_blocks = [times(lblk[LOCAL_COUNT, b], lower).T.astype(BF16) for b in range(2)]
    up_blocks = [times(upper, ublk[0, b]).T.astype(BF16) for b in range(2)]
    up_blocks.append(times(upper, lower).T.astype(BF16))
    for copy in leaf:
        copy.wait()
    for v in range(1, UPPER + 1):
        sums[(v - 1) * RHS : v * RHS] = jnp.where(my_level == v, rights[LOCAL_COUNT], 0.0)
    pending = jnp.zeros((RHS, W), F32)
    for slot in range(LOCAL_COUNT):
        residue = rights[slot]
        if slot == LOCAL_COUNT - 1:
            residue = residue - pending
        forward = jnp.where(
            row_pad(widths[0, slot]), times_rows(residue.astype(BF16), linv[slot]), 0.0
        )
        solved[slot] = forward
        half = forward.astype(BF16)
        near = times_rows(half, lblk[slot, 0])
        away = times_rows(half, lblk[slot, 1])
        if slot == LOCAL_COUNT - 1:
            sums[:RHS] = sums[:RHS] - near
            target = far[0, slot]
        else:
            pending = pending + near
            target = far[0, slot] - 1
        for v in range(1, UPPER + 1):
            rows = slice((v - 1) * RHS, v * RHS)
            sums[rows] = sums[rows] - jnp.where(target == v, away, 0.0)
    halves = sums[...].astype(BF16)

    def write(low, up):
        for b in range(2):
            low[b * W : (b + 1) * W] = low_blocks[b]
        low[FAR_A : FAR_A + RHS] = distance
        low[SUMS : SUMS + UPPER * RHS] = halves
        low[SUMS + UPPER * RHS :] = jnp.zeros((ROWS - SUMS - UPPER * RHS, W), BF16)
        for b in range(3):
            up[b * W : (b + 1) * W] = up_blocks[b]
        up[FAR_B:] = distance

    @pl.when(place % 2 == 0)
    def _():
        write(first, second)

    @pl.when(place % 2 == 1)
    def _():
        write(second, first)


def begin(rights, linv, uinv, lblk, ublk, widths, far, owner):
    return pl.pallas_call(
        begin_kernel,
        in_specs=[HBM] * 7 + [VMEM],
        out_specs=[VMEM] * 6,
        out_shape=[
            jax.ShapeDtypeStruct((ROWS, W), BF16),
            jax.ShapeDtypeStruct((ROWS, W), BF16),
            jax.ShapeDtypeStruct((LOCAL_COUNT, RHS, W), F32),
            jax.ShapeDtypeStruct((UPPER * RHS, W), F32),
            jax.ShapeDtypeStruct((FLAGS * RHS, W), BF16),
            jax.ShapeDtypeStruct((RHS, W), F32),
        ],
        scratch_shapes=[
            pltpu.VMEM((4, RHS, W), F32),
            pltpu.VMEM((4, W, W), BF16),
            pltpu.VMEM((1, W, W), BF16),
            pltpu.VMEM((4, 2, W, W), BF16),
            pltpu.VMEM((1, 2, W, W), BF16),
            pltpu.SMEM((1, 4), jnp.int32),
            pltpu.SMEM((1, 4), jnp.int32),
            pltpu.SemaphoreType.DMA((9,)),
        ],
        compiler_params=BEGIN_PARAMS,
    )(rights, linv, uinv, lblk, ublk, widths, far, owner)


def flag(flags, index):
    return part(flags, index).astype(F32) > 0.5


def choose(test, one, other):
    return jnp.where(test, one.astype(F32), other.astype(F32)).astype(BF16)


def choose_rows(test, one, other, chosen, left):
    wide = jnp.concatenate([test] * 16, axis=0)
    for start in range(0, ROWS, W):
        rows = slice(start, min(start + W, ROWS))
        amount = rows.stop - rows.start
        a, b = (one[rows], other[rows])
        chosen[rows] = choose(wide[:amount], a, b)
        left[rows] = choose(wide[:amount], b, a)


def eliminate(total, low):
    half = total[:RHS].astype(BF16)
    near = times(half, low[:W])
    away = times(half, low[W : 2 * W])
    distance = low[FAR_A : FAR_A + RHS].astype(F32)
    rest = []
    for step in range(1, total.shape[0] // RHS):
        value = part(total, step)
        if step == 1:
            value = value - near
        rest.append(value - jnp.where(distance == float(step), away, 0.0))
    return half, jnp.concatenate(rest, axis=0)


def pass_on(flags, rest, left):
    rows = rest.shape[0]
    wide = jnp.concatenate([flag(flags, ROLE_A)] * (rows // RHS), axis=0)
    left[SUMS : SUMS + rows] = choose(wide, rest.astype(BF16), left[SUMS : SUMS + rows])


def gather_kernel(
    height, own, r1, r2, r3, sums, flags, k1, k1q, k2, left, residues, rest, lp, lq
):
    choose_rows(flag(flags, height - 1), own, r1, k1, lp)
    choose_rows(flag(flags, OTHER_PAIR[height]), r2, r3, k1q, lq)
    choose_rows(flag(flags, height), lp, lq, k2, left)
    rows = slice(SUMS, SUMS + sums.shape[0])
    near = sums[...] + r1[rows].astype(F32)
    other = r2[rows].astype(F32) + r3[rows].astype(F32)
    half, near = eliminate(near, k1)
    residues[:RHS] = half
    half, other = eliminate(other, k1q)
    residues[RHS : 2 * RHS] = half
    half, value = eliminate(near + other, k2)
    residues[2 * RHS :] = half
    rest[...] = value
    pass_on(flags, value, left)


def gather(height, own, came, sums, flags):
    message = jax.ShapeDtypeStruct((ROWS, W), BF16)
    *results, residues, rest = pl.pallas_call(
        functools.partial(gather_kernel, height),
        in_specs=[VMEM] * 6,
        out_specs=[VMEM] * 6,
        out_shape=[message] * 4
        + [
            jax.ShapeDtypeStruct((3 * RHS, W), BF16),
            jax.ShapeDtypeStruct((sums.shape[0] - 2 * RHS, W), F32),
        ],
        scratch_shapes=[pltpu.VMEM((ROWS, W), BF16)] * 2,
        compiler_params=PARAMS,
    )(own, *came, sums, flags)
    return results[:3], results[3], residues, rest


def climb_kernel(height, own, came, sums, flags, chosen, left, residue, rest):
    choose_rows(flag(flags, height - 1), own, came, chosen, left)
    total = sums[...] + came[SUMS : SUMS + sums.shape[0]].astype(F32)
    half, value = eliminate(total, chosen)
    residue[...] = half
    rest[...] = value
    pass_on(flags, value, left)


def climb(height, own, came, sums, flags):
    message = jax.ShapeDtypeStruct((ROWS, W), BF16)
    return pl.pallas_call(
        functools.partial(climb_kernel, height),
        in_specs=[VMEM] * 4,
        out_specs=[VMEM] * 4,
        out_shape=[
            message,
            message,
            jax.ShapeDtypeStruct((RHS, W), BF16),
            jax.ShapeDtypeStruct((sums.shape[0] - RHS, W), F32),
        ],
        compiler_params=PARAMS,
    )(own, came, sums, flags)


def separator(residue, up, above):
    distance = up[FAR_B : FAR_B + RHS].astype(F32)
    known = jnp.zeros((RHS, W), F32)
    for step, value in enumerate(above, 1):
        known = known + jnp.where(distance == float(step), value.astype(F32), 0.0)
    return (
        times(residue, up[2 * W : 3 * W])
        - times(above[0], up[:W])
        - times(known.astype(BF16), up[W : 2 * W])
    ).astype(BF16)


def top_kernel(
    vectors, root, mine, came, flags, u3, u3q, u4, u5, u6, u7, near_out, other_out
):
    wide = jnp.concatenate([flag(flags, UPPER - 1)] * 16, axis=0)
    last = choose(wide, mine[2 * W : 3 * W], came[...])
    residue = part(vectors, 10).astype(F32) + root[...].astype(F32)
    above = [times(residue.astype(BF16), last).astype(BF16)]
    for index, up in ((9, u7), (7, u6), (6, u5), (5, u4)):
        above = [separator(part(vectors, index), up, above)] + above
    for index, up, out in ((3, u3, near_out), (4, u3q, other_out)):
        out[:RHS] = separator(part(vectors, index), up, above)
        for step, value in enumerate(above, 1):
            out[step * RHS : (step + 1) * RHS] = value


def top(vectors, root, mine, came, flags, *ups):
    known = jax.ShapeDtypeStruct(((UPPER - LOW) * RHS, W), BF16)
    return pl.pallas_call(
        top_kernel,
        in_specs=[VMEM] * (5 + len(ups)),
        out_specs=[VMEM] * 2,
        out_shape=[known, known],
        compiler_params=PARAMS,
    )(vectors, root, mine, came, flags, *ups)


def select_known(cases, known):
    for test, ref in cases:

        @pl.when(test)
        def _():
            known[...] = ref[...]


def bottom_kernel(vectors, own, a, b, c, u1, u1q, u2, near_out, other_out, known):
    z = lax.axis_index("col") // 4
    first, last = LEADERS
    select_known(
        [
            ((z == (first ^ k)) | (z == (last ^ k)), ref)
            for k, ref in enumerate((own, a, b, c))
        ],
        known,
    )
    above = [part(known, k) for k in range(UPPER - LOW)]
    above = [separator(part(vectors, 2), u2, above)] + above
    for index, up, out in ((0, u1, near_out), (1, u1q, other_out)):
        out[:RHS] = separator(part(vectors, index), up, above)
        for step, value in enumerate(above, 1):
            out[step * RHS : (step + 1) * RHS] = value


def bottom(vectors, own, a, b, c, u1, u1q, u2):
    known = jax.ShapeDtypeStruct((UPPER * RHS, W), BF16)
    return pl.pallas_call(
        bottom_kernel,
        in_specs=[VMEM] * 8,
        out_specs=[VMEM] * 2,
        out_shape=[known, known],
        scratch_shapes=[pltpu.VMEM(((UPPER - LOW) * RHS, W), BF16)],
        compiler_params=PARAMS,
    )(vectors, own, a, b, c, u1, u1q, u2)


def descend_kernel(
    uinv_in,
    ublk_in,
    widths_in,
    far_in,
    level,
    solved,
    own,
    a,
    b,
    c,
    out,
    uinv,
    ublk,
    widths,
    far,
    known,
    sems,
):
    rest = pl.ds(0, LOCAL_COUNT)
    copies = [
        pltpu.make_async_copy(widths_in, widths, sems.at[0]),
        pltpu.make_async_copy(far_in, far, sems.at[1]),
        pltpu.make_async_copy(uinv_in.at[0, rest], uinv, sems.at[2]),
        pltpu.make_async_copy(ublk_in.at[0, rest], ublk, sems.at[3]),
    ]
    for copy in copies:
        copy.start()
    place = (lax.axis_index("col") % 4 + 2 * lax.axis_index("gz")) % 4
    select_known(
        [(place == seated, ref) for seated, ref in enumerate((a, own, b, c))], known
    )
    above = [part(known, k) for k in range(UPPER)]
    own_value = jnp.zeros((RHS, W), F32)
    for k, value in enumerate(above):
        own_value = jnp.where(level[...] == k + 1, value.astype(F32), own_value)
    out[0, LOCAL_COUNT] = own_value
    for copy in copies:
        copy.wait()
    for slot in (2, 1, 0):
        distant = jnp.zeros((RHS, W), F32)
        for step, value in enumerate(above, 1):
            distant = distant + jnp.where(far[0, slot] == step, value.astype(F32), 0.0)
        residue = (
            solved[slot]
            - times_rows(above[0], ublk[slot, 0])
            - times_rows(distant.astype(BF16), ublk[slot, 1])
        )
        value = jnp.where(
            row_pad(widths[0, slot]), times_rows(residue.astype(BF16), uinv[slot]), 0.0
        )
        out[0, slot] = value
        if slot == 2:
            above = [value.astype(BF16)] + above


def descend(uinv, ublk, widths, far, level, solved, own, a, b, c):
    return pl.pallas_call(
        descend_kernel,
        in_specs=[HBM] * 4 + [VMEM] * 6,
        out_specs=VMEM,
        out_shape=jax.ShapeDtypeStruct((1, 4, RHS, W), F32),
        scratch_shapes=[
            pltpu.VMEM((LOCAL_COUNT, W, W), BF16),
            pltpu.VMEM((LOCAL_COUNT, 2, W, W), BF16),
            pltpu.SMEM((1, 4), jnp.int32),
            pltpu.SMEM((1, 4), jnp.int32),
            pltpu.VMEM((UPPER * RHS, W), BF16),
            pltpu.SemaphoreType.DMA((4,)),
        ],
        compiler_params=PARAMS,
    )(uinv, ublk, widths, far, level, solved, own, a, b, c)


def local(rights, linv, uinv, lblk, ublk, widths, far, owner_level):
    first, second, solved, sums, flags, level = begin(
        rights, linv, uinv, lblk, ublk, widths, far, owner_level.reshape(1, DEVICES)
    )
    came = (
        send(second, seats(((1, 0), (0, 1)))),
        send(first, seats(((2, 0), (3, 1)))),
        send(second, seats(((3, 0), (2, 1)))),
    )
    ups_y, message, residues_y, sums = gather(1, first, came, sums, flags)
    came = [send(message, to_leaders(k)) for k in (1, 2, 3)]
    ups_z, message, residues_z, sums = gather(3, message, came, sums, flags)
    came = send(message, across(4 * (LEADERS[0] ^ LEADERS[1])))
    up_5, message, residue_5, sums = climb(5, message, came, sums, flags)
    came = [send(message, across(32 * k)) for k in (1, 2, 3)]
    ups_x, message, residues_x, sums = gather(6, message, came, sums, flags)
    root = sums.astype(BF16)
    root_came = send(root, layers(0, 1))
    vectors = jnp.concatenate([residues_y, residues_z, residue_5, residues_x, root], axis=0)
    vectors = send(vectors, seats(((0, 1),)))
    last_came = send(message[2 * W : 3 * W], layers(1, 1))
    known, known_other = top(
        vectors, root_came, message, last_came, flags, *ups_z, up_5, ups_x[0], ups_x[2]
    )
    a = send(known, from_leaders(1))
    b = send(known_other, from_leaders(2))
    c = send(known_other, from_leaders(3))
    known, known_other = bottom(vectors, known, a, b, c, *ups_y)
    a = send(known, seats(((1, 0),)))
    b = send(known_other, seats(((1, 2),)))
    c = send(known_other, seats(((1, 3),)))
    return descend(uinv, ublk, widths, far, level, solved, known, a, b, c)


def solution(mesh):
    split = P(AXES)
    in_specs = (split,) * 7 + (P(),)
    return jax.shard_map(local, mesh=mesh, in_specs=in_specs, out_specs=split, check_vma=False)
```

```python
import functools

import jax
import jax.numpy as jnp
from jax import lax
from jax.experimental import pallas as pl
from jax.experimental.pallas import tpu as pltpu
from jax.sharding import PartitionSpec as P

W = 256
RHS = 16
LOCAL_COUNT = 3
UPPER = 8
LOW = 2
DEVICES = 256
AXES = ("gz", "row", "col")
BF16 = jnp.bfloat16
F32 = jnp.float32
FAR_A = 2 * W
SUMS = 2 * W + RHS
FAR_B = 3 * W
ROWS = 3 * W + RHS
GATHERS = (1, 3, 6)
OTHER_PAIR = {low: UPPER + k for k, low in enumerate(GATHERS)}
ROLE_A = UPPER + len(GATHERS)
FLAGS = ROLE_A + 1
LEADERS = (2, 5)
VMEM = pl.BlockSpec(memory_space=pltpu.VMEM)
HBM = pl.BlockSpec(memory_space=pltpu.HBM)
PARAMS = pltpu.CompilerParams(vmem_limit_bytes=24 * 1024 * 1024)


def seat(t):
    return (t % 4 - (0 if t < DEVICES // 2 else 2)) % 4


def at_seat(t, place):
    return t - t % 4 + (place + (0 if t < DEVICES // 2 else 2)) % 4


def send(value, pairs):
    return lax.ppermute(value, AXES, pairs)


def seats(moves):
    firsts = [t for t in range(DEVICES) if t % 4 == 0]
    return [(at_seat(t, a), at_seat(t, b)) for t in firsts for a, b in moves]


def leads(t):
    return seat(t) < 2 and t // 4 % 8 in LEADERS


def to_leaders(distance):
    return [(t ^ (4 * distance), t) for t in range(DEVICES) if leads(t)]


def from_leaders(distance):
    return [(t, t ^ (4 * distance)) for t in range(DEVICES) if leads(t) and seat(t) == 1]


def across(mask):
    return [(t, t ^ mask) for t in range(DEVICES) if leads(t)]


def layers(a, b):
    firsts = [t for t in range(DEVICES) if t % 4 == 0 and t // 4 % 8 in LEADERS]
    return [(at_seat(t, a), at_seat(t ^ (DEVICES // 2), b)) for t in firsts]


def times(vectors, blocks):
    return jnp.dot(vectors, blocks, preferred_element_type=F32)


def times_rows(vectors, blocks):
    return lax.dot_general(
        vectors, blocks, (((1,), (1,)), ((), ())), preferred_element_type=F32
    )


def row_pad(width):
    return lax.broadcasted_iota(jnp.int32, (1, W), 1) < width


def part(rows, index):
    return rows[index * RHS : (index + 1) * RHS]


def begin_kernel(
    rights_in,
    linv_in,
    uinv_in,
    lblk_in,
    ublk_in,
    widths_in,
    far_in,
    owner_in,
    first,
    second,
    solved,
    sums,
    flags,
    level,
    slots,
    rights,
    linv,
    uinv,
    lblk,
    ublk,
    widths,
    far,
    owner,
    sems,
):
    own = pl.ds(LOCAL_COUNT, 1)
    rest = pl.ds(0, LOCAL_COUNT)
    small = [
        pltpu.make_async_copy(widths_in, widths, sems.at[0]),
        pltpu.make_async_copy(far_in, far, sems.at[1]),
    ]
    owner_copy = pltpu.make_async_copy(owner_in, owner, sems.at[9])
    owner_copy.start()
    mine = [
        pltpu.make_async_copy(linv_in.at[0, own], linv.at[own], sems.at[2]),
        pltpu.make_async_copy(lblk_in.at[0, own], lblk.at[own], sems.at[3]),
        pltpu.make_async_copy(uinv_in.at[0, own], uinv, sems.at[4]),
        pltpu.make_async_copy(ublk_in.at[0, own], ublk, sems.at[5]),
    ]
    leaf = [
        pltpu.make_async_copy(rights_in.at[0], rights, sems.at[6]),
        pltpu.make_async_copy(linv_in.at[0, rest], linv.at[rest], sems.at[7]),
        pltpu.make_async_copy(lblk_in.at[0, rest], lblk.at[rest], sems.at[8]),
    ]
    for copy in small + mine + leaf:
        copy.start()
    gz = lax.axis_index("gz")
    col = lax.axis_index("col")
    me = gz * (DEVICES // 2) + lax.axis_index("row") * (DEVICES // 8) + col
    y = col % 4
    place = (y + 2 * gz) % 4
    everyone = lax.broadcasted_iota(jnp.int32, (1, DEVICES), 1)
    owner_copy.wait()
    owners = owner[...]

    def spread(value):
        return jnp.broadcast_to(value, (RHS, W))

    def found(chosen):
        return spread(jnp.max(jnp.where(chosen, 1.0, 0.0), axis=1, keepdims=True))

    for v in range(1, UPPER + 1):
        half = lax.shift_right_logical(everyone, v - 1) == lax.shift_right_logical(me, v - 1)
        flags[(v - 1) * RHS : v * RHS] = found(half & (owners == v)).astype(BF16)
    for v in GATHERS:
        half = lax.shift_right_logical(everyone, v - 1) == (
            lax.shift_right_logical(me, v - 1) ^ 2
        )
        flags[OTHER_PAIR[v] * RHS : (OTHER_PAIR[v] + 1) * RHS] = found(
            half & (owners == v)
        ).astype(BF16)
    flags[ROLE_A * RHS : (ROLE_A + 1) * RHS] = jnp.full(
        (RHS, W), jnp.where(place == 0, 1.0, 0.0), F32
    ).astype(BF16)
    my_level = spread(
        jnp.sum(jnp.where(everyone == me, owners, 0).astype(F32), axis=1, keepdims=True)
    )
    level[...] = my_level
    for copy in small + mine:
        copy.wait()
    pad = lax.broadcasted_iota(jnp.int32, (W, 1), 0) < widths[0, LOCAL_COUNT]
    distance = jnp.full((RHS, W), far[0, LOCAL_COUNT], jnp.int32).astype(F32).astype(BF16)
    lower = jnp.where(pad, linv[LOCAL_COUNT].astype(F32), 0.0).astype(BF16)
    upper = jnp.where(pad, uinv[0].astype(F32), 0.0).astype(BF16)
    low_blocks = [times(lblk[LOCAL_COUNT, b], lower).T.astype(BF16) for b in range(2)]
    up_blocks = [times(upper, ublk[0, b]).T.astype(BF16) for b in range(2)]
    up_blocks.append(times(upper, lower).T.astype(BF16))
    for copy in leaf:
        copy.wait()
    for v in range(1, UPPER + 1):
        sums[(v - 1) * RHS : v * RHS] = jnp.where(my_level == v, rights[LOCAL_COUNT], 0.0)
    pending = jnp.zeros((RHS, W), F32)
    for slot in range(LOCAL_COUNT):
        residue = rights[slot]
        if slot == LOCAL_COUNT - 1:
            residue = residue - pending
        inside = jnp.broadcast_to(row_pad(widths[0, slot]), (RHS, W))
        forward = jnp.where(inside, times_rows(residue.astype(BF16), linv[slot]), 0.0)
        solved[slot] = forward
        slots[slot * RHS : (slot + 1) * RHS] = jnp.where(inside, 1.0, 0.0)
        slots[(LOCAL_COUNT + slot) * RHS : (LOCAL_COUNT + slot + 1) * RHS] = jnp.full(
            (RHS, W), far[0, slot], jnp.int32
        ).astype(F32)
        half = forward.astype(BF16)
        near = times_rows(half, lblk[slot, 0])
        away = times_rows(half, lblk[slot, 1])
        if slot == LOCAL_COUNT - 1:
            sums[:RHS] = sums[:RHS] - near
            target = far[0, slot]
        else:
            pending = pending + near
            target = far[0, slot] - 1
        for v in range(1, UPPER + 1):
            rows = slice((v - 1) * RHS, v * RHS)
            sums[rows] = sums[rows] - jnp.where(target == v, away, 0.0)
    halves = sums[...].astype(BF16)

    def write(low, up):
        for b in range(2):
            low[b * W : (b + 1) * W] = low_blocks[b]
        low[FAR_A : FAR_A + RHS] = distance
        low[SUMS : SUMS + UPPER * RHS] = halves
        low[SUMS + UPPER * RHS :] = jnp.zeros((ROWS - SUMS - UPPER * RHS, W), BF16)
        for b in range(3):
            up[b * W : (b + 1) * W] = up_blocks[b]
        up[FAR_B:] = distance

    @pl.when(place % 2 == 0)
    def _():
        write(first, second)

    @pl.when(place % 2 == 1)
    def _():
        write(second, first)


def begin(rights, linv, uinv, lblk, ublk, widths, far, owner):
    return pl.pallas_call(
        begin_kernel,
        in_specs=[HBM] * 8,
        out_specs=[VMEM] * 7,
        out_shape=[
            jax.ShapeDtypeStruct((ROWS, W), BF16),
            jax.ShapeDtypeStruct((ROWS, W), BF16),
            jax.ShapeDtypeStruct((LOCAL_COUNT, RHS, W), F32),
            jax.ShapeDtypeStruct((UPPER * RHS, W), F32),
            jax.ShapeDtypeStruct((FLAGS * RHS, W), BF16),
            jax.ShapeDtypeStruct((RHS, W), F32),
            jax.ShapeDtypeStruct((2 * LOCAL_COUNT * RHS, W), F32),
        ],
        scratch_shapes=[
            pltpu.VMEM((4, RHS, W), F32),
            pltpu.VMEM((4, W, W), BF16),
            pltpu.VMEM((1, W, W), BF16),
            pltpu.VMEM((4, 2, W, W), BF16),
            pltpu.VMEM((1, 2, W, W), BF16),
            pltpu.SMEM((1, 4), jnp.int32),
            pltpu.SMEM((1, 4), jnp.int32),
            pltpu.VMEM((1, DEVICES), jnp.int32),
            pltpu.SemaphoreType.DMA((10,)),
        ],
        compiler_params=PARAMS,
    )(
        *[
            pltpu.with_memory_space_constraint(value, pltpu.HBM)
            for value in (rights, linv, uinv, lblk, ublk, widths, far, owner)
        ]
    )


def flag(flags, index):
    return part(flags, index).astype(F32) > 0.5


def choose(test, one, other):
    return jnp.where(test, one.astype(F32), other.astype(F32)).astype(BF16)


def choose_rows(test, one, other, chosen, left):
    wide = jnp.concatenate([test] * 16, axis=0)
    for start in range(0, ROWS, W):
        rows = slice(start, min(start + W, ROWS))
        amount = rows.stop - rows.start
        a, b = (one[rows], other[rows])
        chosen[rows] = choose(wide[:amount], a, b)
        left[rows] = choose(wide[:amount], b, a)


def eliminate(total, low):
    half = total[:RHS].astype(BF16)
    near = times(half, low[:W])
    away = times(half, low[W : 2 * W])
    distance = low[FAR_A : FAR_A + RHS].astype(F32)
    rest = []
    for step in range(1, total.shape[0] // RHS):
        value = part(total, step)
        if step == 1:
            value = value - near
        rest.append(value - jnp.where(distance == float(step), away, 0.0))
    return half, jnp.concatenate(rest, axis=0)


def pass_on(flags, rest, left):
    rows = rest.shape[0]
    wide = jnp.concatenate([flag(flags, ROLE_A)] * (rows // RHS), axis=0)
    left[SUMS : SUMS + rows] = choose(wide, rest.astype(BF16), left[SUMS : SUMS + rows])


def gather_kernel(
    height, own, r1, r2, r3, sums, flags, left, residues, rest, k1, k2, k1q, lp, lq
):
    choose_rows(flag(flags, height - 1), own, r1, k1, lp)
    choose_rows(flag(flags, OTHER_PAIR[height]), r2, r3, k1q, lq)
    choose_rows(flag(flags, height), lp, lq, k2, left)
    rows = slice(SUMS, SUMS + sums.shape[0])
    near = sums[...] + r1[rows].astype(F32)
    other = r2[rows].astype(F32) + r3[rows].astype(F32)
    half, near = eliminate(near, k1)
    residues[:RHS] = half
    half, other = eliminate(other, k1q)
    residues[RHS : 2 * RHS] = half
    half, value = eliminate(near + other, k2)
    residues[2 * RHS :] = half
    rest[...] = value
    pass_on(flags, value, left)


def gather(height, own, came, sums, flags, both=True):
    message = jax.ShapeDtypeStruct((ROWS, W), BF16)
    kept = 3 if both else 2
    left, residues, rest, *ups = pl.pallas_call(
        functools.partial(gather_kernel, height),
        in_specs=[VMEM] * 6,
        out_specs=[VMEM] * (3 + kept),
        out_shape=[
            message,
            jax.ShapeDtypeStruct((3 * RHS, W), BF16),
            jax.ShapeDtypeStruct((sums.shape[0] - 2 * RHS, W), F32),
        ]
        + [message] * kept,
        scratch_shapes=[pltpu.VMEM((ROWS, W), BF16)] * (5 - kept),
        compiler_params=PARAMS,
    )(own, *came, sums, flags)
    return ups, left, residues, rest


def climb_kernel(height, own, came, sums, flags, chosen, left, residue, rest):
    choose_rows(flag(flags, height - 1), own, came, chosen, left)
    total = sums[...] + came[SUMS : SUMS + sums.shape[0]].astype(F32)
    half, value = eliminate(total, chosen)
    residue[...] = half
    rest[...] = value
    pass_on(flags, value, left)


def climb(height, own, came, sums, flags):
    message = jax.ShapeDtypeStruct((ROWS, W), BF16)
    return pl.pallas_call(
        functools.partial(climb_kernel, height),
        in_specs=[VMEM] * 4,
        out_specs=[VMEM] * 4,
        out_shape=[
            message,
            message,
            jax.ShapeDtypeStruct((RHS, W), BF16),
            jax.ShapeDtypeStruct((sums.shape[0] - RHS, W), F32),
        ],
        compiler_params=PARAMS,
    )(own, came, sums, flags)


def separator(residue, up, above):
    distance = up[FAR_B : FAR_B + RHS].astype(F32)
    known = jnp.zeros((RHS, W), F32)
    for step, value in enumerate(above, 1):
        known = known + jnp.where(distance == float(step), value.astype(F32), 0.0)
    return (
        times(residue, up[2 * W : 3 * W])
        - times(above[0], up[:W])
        - times(known.astype(BF16), up[W : 2 * W])
    ).astype(BF16)


def top_kernel(
    vectors, root, mine, came, flags, u3, u4, u3q, u5, u6, u7, near_out, other_out
):
    wide = jnp.concatenate([flag(flags, UPPER - 1)] * 16, axis=0)
    last = choose(wide, mine[2 * W : 3 * W], came[...])
    residue = part(vectors, 10).astype(F32) + root[...].astype(F32)
    above = [times(residue.astype(BF16), last).astype(BF16)]
    for index, up in ((9, u7), (7, u6), (6, u5), (5, u4)):
        above = [separator(part(vectors, index), up, above)] + above
    for index, up, out in ((3, u3, near_out), (4, u3q, other_out)):
        out[:RHS] = separator(part(vectors, index), up, above)
        for step, value in enumerate(above, 1):
            out[step * RHS : (step + 1) * RHS] = value


def top(vectors, root, mine, came, flags, *ups):
    known = jax.ShapeDtypeStruct(((UPPER - LOW) * RHS, W), BF16)
    return pl.pallas_call(
        top_kernel,
        in_specs=[VMEM] * (5 + len(ups)),
        out_specs=[VMEM] * 2,
        out_shape=[known, known],
        compiler_params=PARAMS,
    )(vectors, root, mine, came, flags, *ups)


def select_known(cases, known):
    for test, ref in cases:

        @pl.when(test)
        def _():
            known[...] = ref[...]


def bottom_kernel(vectors, own, a, b, c, u1, u2, u1q, near_out, other_out, known):
    z = lax.axis_index("col") // 4
    first, last = LEADERS
    select_known(
        [
            ((z == (first ^ k)) | (z == (last ^ k)), ref)
            for k, ref in enumerate((own, a, b, c))
        ],
        known,
    )
    above = [part(known, k) for k in range(UPPER - LOW)]
    above = [separator(part(vectors, 2), u2, above)] + above
    for index, up, out in ((0, u1, near_out), (1, u1q, other_out)):
        out[:RHS] = separator(part(vectors, index), up, above)
        for step, value in enumerate(above, 1):
            out[step * RHS : (step + 1) * RHS] = value


def bottom(vectors, own, a, b, c, u1, u2, u1q):
    known = jax.ShapeDtypeStruct((UPPER * RHS, W), BF16)
    return pl.pallas_call(
        bottom_kernel,
        in_specs=[VMEM] * 8,
        out_specs=[VMEM] * 2,
        out_shape=[known, known],
        scratch_shapes=[pltpu.VMEM(((UPPER - LOW) * RHS, W), BF16)],
        compiler_params=PARAMS,
    )(vectors, own, a, b, c, u1, u2, u1q)


def descend_kernel(uinv, ublk, slots, level, solved, own, a, b, c, out, known):
    place = (lax.axis_index("col") % 4 + 2 * lax.axis_index("gz")) % 4
    select_known(
        [(place == seated, ref) for seated, ref in enumerate((a, own, b, c))], known
    )
    above = [part(known, k) for k in range(UPPER)]
    own_value = jnp.zeros((RHS, W), F32)
    for k, value in enumerate(above):
        own_value = jnp.where(level[...] == float(k + 1), value.astype(F32), own_value)
    out[0, LOCAL_COUNT] = own_value
    for slot in (2, 1, 0):
        distance = part(slots, LOCAL_COUNT + slot)
        distant = jnp.zeros((RHS, W), F32)
        for step, value in enumerate(above, 1):
            distant = distant + jnp.where(distance == float(step), value.astype(F32), 0.0)
        residue = (
            solved[slot]
            - times_rows(above[0], ublk[0, slot, 0])
            - times_rows(distant.astype(BF16), ublk[0, slot, 1])
        )
        value = jnp.where(
            part(slots, slot) > 0.5, times_rows(residue.astype(BF16), uinv[0, slot]), 0.0
        )
        out[0, slot] = value
        if slot == 2:
            above = [value.astype(BF16)] + above


def descend(uinv, ublk, slots, level, solved, own, a, b, c):
    return pl.pallas_call(
        descend_kernel,
        in_specs=[VMEM] * 9,
        out_specs=VMEM,
        out_shape=jax.ShapeDtypeStruct((1, 4, RHS, W), F32),
        scratch_shapes=[pltpu.VMEM((UPPER * RHS, W), BF16)],
        compiler_params=PARAMS,
    )(uinv, ublk, slots, level, solved, own, a, b, c)


def local(rights, linv, uinv, lblk, ublk, widths, far, owner_level):
    first, second, solved, sums, flags, level, slots = begin(
        rights, linv, uinv, lblk, ublk, widths, far, owner_level.reshape(1, DEVICES)
    )
    came = (
        send(second, seats(((1, 0), (0, 1)))),
        send(first, seats(((2, 0), (3, 1)))),
        send(second, seats(((3, 0), (2, 1)))),
    )
    ups_y, message, residues_y, sums = gather(1, first, came, sums, flags)
    came = [send(message, to_leaders(k)) for k in (1, 2, 3)]
    ups_z, message, residues_z, sums = gather(3, message, came, sums, flags)
    came = send(message, across(4 * (LEADERS[0] ^ LEADERS[1])))
    up_5, message, residue_5, sums = climb(5, message, came, sums, flags)
    came = [send(message, across(32 * k)) for k in (1, 2, 3)]
    ups_x, message, residues_x, sums = gather(6, message, came, sums, flags, False)
    root = sums.astype(BF16)
    root_came = send(root, layers(0, 1))
    vectors = jnp.concatenate([residues_y, residues_z, residue_5, residues_x, root], axis=0)
    vectors = send(vectors, seats(((0, 1),)))
    last_came = send(message[2 * W : 3 * W], layers(1, 1))
    known, known_other = top(
        vectors, root_came, message, last_came, flags, *ups_z, up_5, *ups_x
    )
    a = send(known, from_leaders(1))
    b = send(known_other, from_leaders(2))
    c = send(known_other, from_leaders(3))
    known, known_other = bottom(vectors, known, a, b, c, *ups_y)
    a = send(known, seats(((1, 0),)))
    b = send(known_other, seats(((1, 2),)))
    c = send(known_other, seats(((1, 3),)))
    return descend(uinv, ublk, slots, level, solved, known, a, b, c)


def solution(mesh):
    split = P(AXES)
    in_specs = (split,) * 7 + (P(),)
    return jax.shard_map(local, mesh=mesh, in_specs=in_specs, out_specs=split, check_vma=False)
```

```python
import functools

import jax
import jax.numpy as jnp
from jax import lax
from jax.experimental import pallas as pl
from jax.experimental.pallas import tpu as pltpu
from jax.sharding import PartitionSpec as P

W = 256
RHS = 16
LOCAL_COUNT = 3
UPPER = 8
LOW = 2
DEVICES = 256
AXES = ("gz", "row", "col")
BF16 = jnp.bfloat16
F32 = jnp.float32
FAR_A = 2 * W
SUMS = 2 * W + RHS
FAR_B = 3 * W
ROWS = 3 * W + RHS
GATHERS = (1, 3, 6)
OTHER_PAIR = {low: UPPER + k for k, low in enumerate(GATHERS)}
ROLE_A = UPPER + len(GATHERS)
FLAGS = ROLE_A + 1
LEADERS = (2, 5)
VMEM = pl.BlockSpec(memory_space=pltpu.VMEM)
HBM = pl.BlockSpec(memory_space=pltpu.HBM)
PARAMS = pltpu.CompilerParams(vmem_limit_bytes=24 * 1024 * 1024)


def seat(t):
    return (t % 4 - (0 if t < DEVICES // 2 else 2)) % 4


def at_seat(t, place):
    return t - t % 4 + (place + (0 if t < DEVICES // 2 else 2)) % 4


def send(value, pairs):
    return lax.ppermute(value, AXES, pairs)


def seats(moves):
    firsts = [t for t in range(DEVICES) if t % 4 == 0]
    return [(at_seat(t, a), at_seat(t, b)) for t in firsts for a, b in moves]


def leads(t):
    return seat(t) < 2 and t // 4 % 8 in LEADERS


def to_leaders(distance):
    return [(t ^ (4 * distance), t) for t in range(DEVICES) if leads(t)]


def from_leaders(distance):
    return [(t, t ^ (4 * distance)) for t in range(DEVICES) if leads(t) and seat(t) == 1]


def across(mask):
    return [(t, t ^ mask) for t in range(DEVICES) if leads(t)]


def layers(a, b):
    firsts = [t for t in range(DEVICES) if t % 4 == 0 and t // 4 % 8 in LEADERS]
    return [(at_seat(t, a), at_seat(t ^ (DEVICES // 2), b)) for t in firsts]


def times(vectors, blocks):
    return jnp.dot(vectors, blocks, preferred_element_type=F32)


def times_rows(vectors, blocks):
    return lax.dot_general(
        vectors, blocks, (((1,), (1,)), ((), ())), preferred_element_type=F32
    )


def row_pad(width):
    return lax.broadcasted_iota(jnp.int32, (1, W), 1) < width


def part(rows, index):
    return rows[index * RHS : (index + 1) * RHS]


def begin_kernel(
    rights_in,
    linv_in,
    uinv_in,
    lblk_in,
    ublk_in,
    widths_in,
    far_in,
    owner_in,
    first,
    second,
    solved,
    sums,
    flags,
    level,
    slots,
    rights,
    linv,
    uinv,
    lblk,
    ublk,
    widths,
    far,
    owner,
    sems,
):
    own = pl.ds(LOCAL_COUNT, 1)
    rest = pl.ds(0, LOCAL_COUNT)
    small = [
        pltpu.make_async_copy(widths_in, widths, sems.at[0]),
        pltpu.make_async_copy(far_in, far, sems.at[1]),
    ]
    owner_copy = pltpu.make_async_copy(owner_in, owner, sems.at[9])
    owner_copy.start()
    mine = [
        pltpu.make_async_copy(linv_in.at[0, own], linv.at[own], sems.at[2]),
        pltpu.make_async_copy(lblk_in.at[0, own], lblk.at[own], sems.at[3]),
        pltpu.make_async_copy(uinv_in.at[0, own], uinv, sems.at[4]),
        pltpu.make_async_copy(ublk_in.at[0, own], ublk, sems.at[5]),
    ]
    leaf = [
        pltpu.make_async_copy(rights_in.at[0], rights, sems.at[6]),
        pltpu.make_async_copy(linv_in.at[0, rest], linv.at[rest], sems.at[7]),
        pltpu.make_async_copy(lblk_in.at[0, rest], lblk.at[rest], sems.at[8]),
    ]
    for copy in small + mine + leaf:
        copy.start()
    gz = lax.axis_index("gz")
    col = lax.axis_index("col")
    me = gz * (DEVICES // 2) + lax.axis_index("row") * (DEVICES // 8) + col
    y = col % 4
    place = (y + 2 * gz) % 4
    everyone = lax.broadcasted_iota(jnp.int32, (1, DEVICES), 1)
    owner_copy.wait()
    owners = owner[...]

    def spread(value):
        return jnp.broadcast_to(value, (RHS, W))

    def found(chosen):
        return spread(jnp.max(jnp.where(chosen, 1.0, 0.0), axis=1, keepdims=True))

    for v in range(1, UPPER + 1):
        half = lax.shift_right_logical(everyone, v - 1) == lax.shift_right_logical(me, v - 1)
        flags[(v - 1) * RHS : v * RHS] = found(half & (owners == v)).astype(BF16)
    for v in GATHERS:
        half = lax.shift_right_logical(everyone, v - 1) == (
            lax.shift_right_logical(me, v - 1) ^ 2
        )
        flags[OTHER_PAIR[v] * RHS : (OTHER_PAIR[v] + 1) * RHS] = found(
            half & (owners == v)
        ).astype(BF16)
    flags[ROLE_A * RHS : (ROLE_A + 1) * RHS] = jnp.full(
        (RHS, W), jnp.where(place == 0, 1.0, 0.0), F32
    ).astype(BF16)
    my_level = spread(
        jnp.sum(jnp.where(everyone == me, owners, 0).astype(F32), axis=1, keepdims=True)
    )
    level[...] = my_level
    for copy in small + mine:
        copy.wait()
    pad = lax.broadcasted_iota(jnp.int32, (W, 1), 0) < widths[0, LOCAL_COUNT]
    distance = jnp.full((RHS, W), far[0, LOCAL_COUNT], jnp.int32).astype(F32).astype(BF16)
    lower = jnp.where(pad, linv[LOCAL_COUNT].astype(F32), 0.0).astype(BF16)
    upper = jnp.where(pad, uinv[0].astype(F32), 0.0).astype(BF16)
    low_blocks = [times(lblk[LOCAL_COUNT, b], lower).T.astype(BF16) for b in range(2)]
    up_blocks = [times(upper, ublk[0, b]).T.astype(BF16) for b in range(2)]
    up_blocks.append(times(upper, lower).T.astype(BF16))
    for copy in leaf:
        copy.wait()
    for v in range(1, UPPER + 1):
        sums[(v - 1) * RHS : v * RHS] = jnp.where(my_level == v, rights[LOCAL_COUNT], 0.0)
    pending = jnp.zeros((RHS, W), F32)
    for slot in range(LOCAL_COUNT):
        residue = rights[slot]
        if slot == LOCAL_COUNT - 1:
            residue = residue - pending
        inside = jnp.broadcast_to(row_pad(widths[0, slot]), (RHS, W))
        forward = jnp.where(inside, times_rows(residue.astype(BF16), linv[slot]), 0.0)
        solved[slot] = forward
        slots[slot * RHS : (slot + 1) * RHS] = jnp.where(inside, 1.0, 0.0)
        slots[(LOCAL_COUNT + slot) * RHS : (LOCAL_COUNT + slot + 1) * RHS] = jnp.full(
            (RHS, W), far[0, slot], jnp.int32
        ).astype(F32)
        half = forward.astype(BF16)
        near = times_rows(half, lblk[slot, 0])
        away = times_rows(half, lblk[slot, 1])
        if slot == LOCAL_COUNT - 1:
            sums[:RHS] = sums[:RHS] - near
            target = far[0, slot]
        else:
            pending = pending + near
            target = far[0, slot] - 1
        for v in range(1, UPPER + 1):
            rows = slice((v - 1) * RHS, v * RHS)
            sums[rows] = sums[rows] - jnp.where(target == v, away, 0.0)
    halves = sums[...].astype(BF16)

    def write(low, up):
        wide = jnp.concatenate([my_level] * (W // RHS), axis=0)
        low[:W] = jnp.where(
            wide == float(UPPER), up_blocks[2].astype(F32), low_blocks[0].astype(F32)
        ).astype(BF16)
        low[W : 2 * W] = low_blocks[1]
        low[FAR_A : FAR_A + RHS] = distance
        low[SUMS : SUMS + UPPER * RHS] = halves
        low[SUMS + UPPER * RHS :] = jnp.zeros((ROWS - SUMS - UPPER * RHS, W), BF16)
        for b in range(3):
            up[b * W : (b + 1) * W] = up_blocks[b]
        up[FAR_B:] = distance

    @pl.when(place % 2 == 0)
    def _():
        write(first, second)

    @pl.when(place % 2 == 1)
    def _():
        write(second, first)


def begin(rights, linv, uinv, lblk, ublk, widths, far, owner):
    return pl.pallas_call(
        begin_kernel,
        in_specs=[HBM] * 8,
        out_specs=[VMEM] * 7,
        out_shape=[
            jax.ShapeDtypeStruct((ROWS, W), BF16),
            jax.ShapeDtypeStruct((ROWS, W), BF16),
            jax.ShapeDtypeStruct((LOCAL_COUNT, RHS, W), F32),
            jax.ShapeDtypeStruct((UPPER * RHS, W), F32),
            jax.ShapeDtypeStruct((FLAGS * RHS, W), BF16),
            jax.ShapeDtypeStruct((RHS, W), F32),
            jax.ShapeDtypeStruct((2 * LOCAL_COUNT * RHS, W), F32),
        ],
        scratch_shapes=[
            pltpu.VMEM((4, RHS, W), F32),
            pltpu.VMEM((4, W, W), BF16),
            pltpu.VMEM((1, W, W), BF16),
            pltpu.VMEM((4, 2, W, W), BF16),
            pltpu.VMEM((1, 2, W, W), BF16),
            pltpu.SMEM((1, 4), jnp.int32),
            pltpu.SMEM((1, 4), jnp.int32),
            pltpu.VMEM((1, DEVICES), jnp.int32),
            pltpu.SemaphoreType.DMA((10,)),
        ],
        compiler_params=PARAMS,
    )(
        *[
            pltpu.with_memory_space_constraint(value, pltpu.HBM)
            for value in (rights, linv, uinv, lblk, ublk, widths, far, owner)
        ]
    )


def flag(flags, index):
    return part(flags, index).astype(F32) > 0.5


def choose(test, one, other):
    return jnp.where(test, one.astype(F32), other.astype(F32)).astype(BF16)


def choose_rows(test, one, other, chosen, left):
    wide = jnp.concatenate([test] * 16, axis=0)
    for start in range(0, ROWS, W):
        rows = slice(start, min(start + W, ROWS))
        amount = rows.stop - rows.start
        a, b = (one[rows], other[rows])
        chosen[rows] = choose(wide[:amount], a, b)
        left[rows] = choose(wide[:amount], b, a)


def eliminate(total, low):
    half = total[:RHS].astype(BF16)
    near = times(half, low[:W])
    away = times(half, low[W : 2 * W])
    distance = low[FAR_A : FAR_A + RHS].astype(F32)
    rest = []
    for step in range(1, total.shape[0] // RHS):
        value = part(total, step)
        if step == 1:
            value = value - near
        rest.append(value - jnp.where(distance == float(step), away, 0.0))
    return half, jnp.concatenate(rest, axis=0)


def pass_on(flags, rest, left):
    rows = rest.shape[0]
    wide = jnp.concatenate([flag(flags, ROLE_A)] * (rows // RHS), axis=0)
    left[SUMS : SUMS + rows] = choose(wide, rest.astype(BF16), left[SUMS : SUMS + rows])


def gather_kernel(
    height, own, r2, r1, r3, sums, flags, left, residues, rest, k1, k2, k1q, lp, lq
):
    choose_rows(flag(flags, height - 1), own, r1, k1, lp)
    choose_rows(flag(flags, OTHER_PAIR[height]), r2, r3, k1q, lq)
    choose_rows(flag(flags, height), lp, lq, k2, left)
    rows = slice(SUMS, SUMS + sums.shape[0])
    near = sums[...] + r1[rows].astype(F32)
    other = r2[rows].astype(F32) + r3[rows].astype(F32)
    half, near = eliminate(near, k1)
    residues[:RHS] = half
    half, other = eliminate(other, k1q)
    residues[RHS : 2 * RHS] = half
    half, value = eliminate(near + other, k2)
    residues[2 * RHS :] = half
    rest[...] = value
    pass_on(flags, value, left)


def gather(height, own, came, sums, flags, both=True):
    message = jax.ShapeDtypeStruct((ROWS, W), BF16)
    kept = 3 if both else 2
    left, residues, rest, *ups = pl.pallas_call(
        functools.partial(gather_kernel, height),
        in_specs=[VMEM] * 6,
        out_specs=[VMEM] * (3 + kept),
        out_shape=[
            message,
            jax.ShapeDtypeStruct((3 * RHS, W), BF16),
            jax.ShapeDtypeStruct((sums.shape[0] - 2 * RHS, W), F32),
        ]
        + [message] * kept,
        scratch_shapes=[pltpu.VMEM((ROWS, W), BF16)] * (5 - kept),
        compiler_params=PARAMS,
    )(own, came[1], came[0], came[2], sums, flags)
    return ups, left, residues, rest


def climb_kernel(height, own, came, sums, flags, chosen, left, residue, rest):
    choose_rows(flag(flags, height - 1), own, came, chosen, left)
    total = sums[...] + came[SUMS : SUMS + sums.shape[0]].astype(F32)
    half, value = eliminate(total, chosen)
    residue[...] = half
    rest[...] = value
    pass_on(flags, value, left)


def climb(height, own, came, sums, flags):
    message = jax.ShapeDtypeStruct((ROWS, W), BF16)
    return pl.pallas_call(
        functools.partial(climb_kernel, height),
        in_specs=[VMEM] * 4,
        out_specs=[VMEM] * 4,
        out_shape=[
            message,
            message,
            jax.ShapeDtypeStruct((RHS, W), BF16),
            jax.ShapeDtypeStruct((sums.shape[0] - RHS, W), F32),
        ],
        compiler_params=PARAMS,
    )(own, came, sums, flags)


def separator(residue, up, above):
    distance = up[FAR_B : FAR_B + RHS].astype(F32)
    known = jnp.zeros((RHS, W), F32)
    for step, value in enumerate(above, 1):
        known = known + jnp.where(distance == float(step), value.astype(F32), 0.0)
    return (
        times(residue, up[2 * W : 3 * W])
        - times(above[0], up[:W])
        - times(known.astype(BF16), up[W : 2 * W])
    ).astype(BF16)


def top_kernel(
    vectors, came, mine, flags, u3, u4, u3q, u5, u6, u7, near_out, other_out
):
    wide = jnp.concatenate([flag(flags, UPPER - 1)] * 16, axis=0)
    last = choose(wide, mine[2 * W : 3 * W], came[:W])
    residue = part(vectors, 10).astype(F32) + came[W:].astype(F32)
    above = [times(residue.astype(BF16), last).astype(BF16)]
    for index, up in ((9, u7), (7, u6), (6, u5), (5, u4)):
        above = [separator(part(vectors, index), up, above)] + above
    for index, up, out in ((3, u3, near_out), (4, u3q, other_out)):
        out[:RHS] = separator(part(vectors, index), up, above)
        for step, value in enumerate(above, 1):
            out[step * RHS : (step + 1) * RHS] = value


def top(vectors, came, mine, flags, *ups):
    known = jax.ShapeDtypeStruct(((UPPER - LOW) * RHS, W), BF16)
    return pl.pallas_call(
        top_kernel,
        in_specs=[VMEM] * (4 + len(ups)),
        out_specs=[VMEM] * 2,
        out_shape=[known, known],
        compiler_params=PARAMS,
    )(vectors, came, mine, flags, *ups)


def select_known(cases, known):
    for test, ref in cases:

        @pl.when(test)
        def _():
            known[...] = ref[...]


def bottom_kernel(vectors, own, a, b, c, u1, u2, u1q, near_out, other_out, known):
    z = lax.axis_index("col") // 4
    first, last = LEADERS
    select_known(
        [
            ((z == (first ^ k)) | (z == (last ^ k)), ref)
            for k, ref in enumerate((own, a, b, c))
        ],
        known,
    )
    above = [part(known, k) for k in range(UPPER - LOW)]
    above = [separator(part(vectors, 2), u2, above)] + above
    for index, up, out in ((0, u1, near_out), (1, u1q, other_out)):
        out[:RHS] = separator(part(vectors, index), up, above)
        for step, value in enumerate(above, 1):
            out[step * RHS : (step + 1) * RHS] = value


def bottom(vectors, own, a, b, c, u1, u2, u1q):
    known = jax.ShapeDtypeStruct((UPPER * RHS, W), BF16)
    return pl.pallas_call(
        bottom_kernel,
        in_specs=[VMEM] * 8,
        out_specs=[VMEM] * 2,
        out_shape=[known, known],
        scratch_shapes=[pltpu.VMEM(((UPPER - LOW) * RHS, W), BF16)],
        compiler_params=PARAMS,
    )(vectors, own, a, b, c, u1, u2, u1q)


def descend_kernel(uinv, ublk, slots, level, solved, own, a, b, c, out, known):
    place = (lax.axis_index("col") % 4 + 2 * lax.axis_index("gz")) % 4
    select_known(
        [(place == seated, ref) for seated, ref in enumerate((a, own, b, c))], known
    )
    above = [part(known, k) for k in range(UPPER)]
    own_value = jnp.zeros((RHS, W), F32)
    for k, value in enumerate(above):
        own_value = jnp.where(level[...] == float(k + 1), value.astype(F32), own_value)
    out[0, LOCAL_COUNT] = own_value
    for slot in (2, 1, 0):
        distance = part(slots, LOCAL_COUNT + slot)
        distant = jnp.zeros((RHS, W), F32)
        for step, value in enumerate(above, 1):
            distant = distant + jnp.where(distance == float(step), value.astype(F32), 0.0)
        residue = (
            solved[slot]
            - times_rows(above[0], ublk[0, slot, 0])
            - times_rows(distant.astype(BF16), ublk[0, slot, 1])
        )
        value = jnp.where(
            part(slots, slot) > 0.5, times_rows(residue.astype(BF16), uinv[0, slot]), 0.0
        )
        out[0, slot] = value
        if slot == 2:
            above = [value.astype(BF16)] + above


def descend(uinv, ublk, slots, level, solved, own, a, b, c):
    return pl.pallas_call(
        descend_kernel,
        in_specs=[VMEM] * 9,
        out_specs=VMEM,
        out_shape=jax.ShapeDtypeStruct((1, 4, RHS, W), F32),
        scratch_shapes=[pltpu.VMEM((UPPER * RHS, W), BF16)],
        compiler_params=PARAMS,
    )(uinv, ublk, slots, level, solved, own, a, b, c)


def local(rights, linv, uinv, lblk, ublk, widths, far, owner_level):
    first, second, solved, sums, flags, level, slots = begin(
        rights, linv, uinv, lblk, ublk, widths, far, owner_level.reshape(1, DEVICES)
    )
    r2 = send(first, seats(((2, 0), (3, 1))))
    r1 = send(second, seats(((1, 0), (0, 1))))
    r3 = send(second, seats(((3, 0), (2, 1))))
    came = (r1, r2, r3)
    ups_y, message, residues_y, sums = gather(1, first, came, sums, flags)
    came = [send(message, to_leaders(k)) for k in (1, 2, 3)]
    ups_z, message, residues_z, sums = gather(3, message, came, sums, flags)
    came = send(message, across(4 * (LEADERS[0] ^ LEADERS[1])))
    up_5, message, residue_5, sums = climb(5, message, came, sums, flags)
    came = {k: send(message, across(32 * k)) for k in (2, 1, 3)}
    came = [came[k] for k in (1, 2, 3)]
    ups_x, message, residues_x, sums = gather(6, message, came, sums, flags, False)
    root = sums.astype(BF16)
    across_came = send(jnp.concatenate([message[:W], root], axis=0), layers(0, 1))
    vectors = jnp.concatenate([residues_y, residues_z, residue_5, residues_x, root], axis=0)
    vectors = send(vectors, seats(((0, 1),)))
    known, known_other = top(
        vectors, across_came, message, flags, *ups_z, up_5, *ups_x
    )
    a = send(known, from_leaders(1))
    b = send(known_other, from_leaders(2))
    c = send(known_other, from_leaders(3))
    known, known_other = bottom(vectors, known, a, b, c, *ups_y)
    a = send(known, seats(((1, 0),)))
    b = send(known_other, seats(((1, 2),)))
    c = send(known_other, seats(((1, 3),)))
    return descend(uinv, ublk, slots, level, solved, known, a, b, c)


def solution(mesh):
    split = P(AXES)
    in_specs = (split,) * 7 + (P(),)
    return jax.shard_map(local, mesh=mesh, in_specs=in_specs, out_specs=split, check_vma=False)
```

```python
import functools

import jax
import jax.numpy as jnp
from jax import lax
from jax.experimental import pallas as pl
from jax.experimental.pallas import tpu as pltpu
from jax.sharding import PartitionSpec as P

W = 256
RHS = 16
LOCAL_COUNT = 3
UPPER = 8
LOW = 2
DEVICES = 256
AXES = ("gz", "row", "col")
BF16 = jnp.bfloat16
F32 = jnp.float32
SHARE = 64
FAR_A = 2 * W
GAIN_A = FAR_A + RHS
SUMS = GAIN_A + SHARE
GAIN_B = 2 * W
FAR_B = GAIN_B + W - SHARE
ROWS = FAR_B + RHS
GATHERS = (1, 3, 6)
OTHER_PAIR = {low: UPPER + k for k, low in enumerate(GATHERS)}
ROLE_A = UPPER + len(GATHERS)
FLAGS = ROLE_A + 1
LEADERS = (2, 5)
VMEM = pl.BlockSpec(memory_space=pltpu.VMEM)
HBM = pl.BlockSpec(memory_space=pltpu.HBM)
PARAMS = pltpu.CompilerParams(vmem_limit_bytes=24 * 1024 * 1024)


def seat(t):
    return (t % 4 - (0 if t < DEVICES // 2 else 2)) % 4


def at_seat(t, place):
    return t - t % 4 + (place + (0 if t < DEVICES // 2 else 2)) % 4


def send(value, pairs):
    return lax.ppermute(value, AXES, pairs)


def seats(moves):
    firsts = [t for t in range(DEVICES) if t % 4 == 0]
    return [(at_seat(t, a), at_seat(t, b)) for t in firsts for a, b in moves]


def leads(t):
    return seat(t) < 2 and t // 4 % 8 in LEADERS


def to_leaders(distance):
    return [(t ^ (4 * distance), t) for t in range(DEVICES) if leads(t)]


def from_leaders(distance):
    return [(t, t ^ (4 * distance)) for t in range(DEVICES) if leads(t) and seat(t) == 1]


def across(mask):
    return [(t, t ^ mask) for t in range(DEVICES) if leads(t)]


def layers(a, b):
    firsts = [t for t in range(DEVICES) if t % 4 == 0 and t // 4 % 8 in LEADERS]
    return [(at_seat(t, a), at_seat(t ^ (DEVICES // 2), b)) for t in firsts]


def times(vectors, blocks):
    return jnp.dot(vectors, blocks, preferred_element_type=F32)


def times_rows(vectors, blocks):
    return lax.dot_general(
        vectors, blocks, (((1,), (1,)), ((), ())), preferred_element_type=F32
    )


def row_pad(width):
    return lax.broadcasted_iota(jnp.int32, (1, W), 1) < width


def part(rows, index):
    return rows[index * RHS : (index + 1) * RHS]


def begin_kernel(
    rights_in,
    linv_in,
    uinv_in,
    lblk_in,
    ublk_in,
    widths_in,
    far_in,
    owner_in,
    first,
    second,
    solved,
    sums,
    flags,
    level,
    slots,
    rights,
    linv,
    uinv,
    lblk,
    ublk,
    widths,
    far,
    owner,
    sems,
):
    own = pl.ds(LOCAL_COUNT, 1)
    rest = pl.ds(0, LOCAL_COUNT)
    small = [
        pltpu.make_async_copy(widths_in, widths, sems.at[0]),
        pltpu.make_async_copy(far_in, far, sems.at[1]),
    ]
    owner_copy = pltpu.make_async_copy(owner_in, owner, sems.at[9])
    owner_copy.start()
    mine = [
        pltpu.make_async_copy(linv_in.at[0, own], linv.at[own], sems.at[2]),
        pltpu.make_async_copy(lblk_in.at[0, own], lblk.at[own], sems.at[3]),
        pltpu.make_async_copy(uinv_in.at[0, own], uinv, sems.at[4]),
        pltpu.make_async_copy(ublk_in.at[0, own], ublk, sems.at[5]),
    ]
    leaf = [
        pltpu.make_async_copy(rights_in.at[0], rights, sems.at[6]),
        pltpu.make_async_copy(linv_in.at[0, rest], linv.at[rest], sems.at[7]),
        pltpu.make_async_copy(lblk_in.at[0, rest], lblk.at[rest], sems.at[8]),
    ]
    for copy in small + mine + leaf:
        copy.start()
    gz = lax.axis_index("gz")
    col = lax.axis_index("col")
    me = gz * (DEVICES // 2) + lax.axis_index("row") * (DEVICES // 8) + col
    y = col % 4
    place = (y + 2 * gz) % 4
    everyone = lax.broadcasted_iota(jnp.int32, (1, DEVICES), 1)
    owner_copy.wait()
    owners = owner[...]

    def spread(value):
        return jnp.broadcast_to(value, (RHS, W))

    def found(chosen):
        return spread(jnp.max(jnp.where(chosen, 1.0, 0.0), axis=1, keepdims=True))

    for v in range(1, UPPER + 1):
        half = lax.shift_right_logical(everyone, v - 1) == lax.shift_right_logical(me, v - 1)
        flags[(v - 1) * RHS : v * RHS] = found(half & (owners == v)).astype(BF16)
    for v in GATHERS:
        half = lax.shift_right_logical(everyone, v - 1) == (
            lax.shift_right_logical(me, v - 1) ^ 2
        )
        flags[OTHER_PAIR[v] * RHS : (OTHER_PAIR[v] + 1) * RHS] = found(
            half & (owners == v)
        ).astype(BF16)
    flags[ROLE_A * RHS : (ROLE_A + 1) * RHS] = jnp.full(
        (RHS, W), jnp.where(place == 0, 1.0, 0.0), F32
    ).astype(BF16)
    my_level = spread(
        jnp.sum(jnp.where(everyone == me, owners, 0).astype(F32), axis=1, keepdims=True)
    )
    level[...] = my_level
    for copy in small + mine:
        copy.wait()
    pad = lax.broadcasted_iota(jnp.int32, (W, 1), 0) < widths[0, LOCAL_COUNT]
    distance = jnp.full((RHS, W), far[0, LOCAL_COUNT], jnp.int32).astype(F32).astype(BF16)
    lower = jnp.where(pad, linv[LOCAL_COUNT].astype(F32), 0.0).astype(BF16)
    upper = jnp.where(pad, uinv[0].astype(F32), 0.0).astype(BF16)
    low_blocks = [times(lblk[LOCAL_COUNT, b], lower).T.astype(BF16) for b in range(2)]
    up_blocks = [times(upper, ublk[0, b]).T.astype(BF16) for b in range(2)]
    up_blocks.append(times(upper, lower).T.astype(BF16))
    for copy in leaf:
        copy.wait()
    for v in range(1, UPPER + 1):
        sums[(v - 1) * RHS : v * RHS] = jnp.where(my_level == v, rights[LOCAL_COUNT], 0.0)
    pending = jnp.zeros((RHS, W), F32)
    for slot in range(LOCAL_COUNT):
        residue = rights[slot]
        if slot == LOCAL_COUNT - 1:
            residue = residue - pending
        inside = jnp.broadcast_to(row_pad(widths[0, slot]), (RHS, W))
        forward = jnp.where(inside, times_rows(residue.astype(BF16), linv[slot]), 0.0)
        solved[slot] = forward
        slots[slot * RHS : (slot + 1) * RHS] = jnp.where(inside, 1.0, 0.0)
        slots[(LOCAL_COUNT + slot) * RHS : (LOCAL_COUNT + slot + 1) * RHS] = jnp.full(
            (RHS, W), far[0, slot], jnp.int32
        ).astype(F32)
        half = forward.astype(BF16)
        near = times_rows(half, lblk[slot, 0])
        away = times_rows(half, lblk[slot, 1])
        if slot == LOCAL_COUNT - 1:
            sums[:RHS] = sums[:RHS] - near
            target = far[0, slot]
        else:
            pending = pending + near
            target = far[0, slot] - 1
        for v in range(1, UPPER + 1):
            rows = slice((v - 1) * RHS, v * RHS)
            sums[rows] = sums[rows] - jnp.where(target == v, away, 0.0)
    halves = sums[...].astype(BF16)

    def write(low, up):
        wide = jnp.concatenate([my_level] * (W // RHS), axis=0) == float(UPPER)
        low[:W] = choose(wide, up_blocks[2], low_blocks[0])
        low[W : 2 * W] = low_blocks[1]
        low[FAR_A:GAIN_A] = distance
        low[GAIN_A:SUMS] = up_blocks[2][:SHARE]
        low[SUMS:] = halves
        up[:SHARE] = choose(wide[:SHARE], up_blocks[2][:SHARE], up_blocks[0][:SHARE])
        up[SHARE:W] = up_blocks[0][SHARE:]
        up[W : 2 * W] = up_blocks[1]
        up[GAIN_B:FAR_B] = up_blocks[2][SHARE:]
        up[FAR_B:] = distance

    @pl.when(place % 2 == 0)
    def _():
        write(first, second)

    @pl.when(place % 2 == 1)
    def _():
        write(second, first)


def begin(rights, linv, uinv, lblk, ublk, widths, far, owner):
    return pl.pallas_call(
        begin_kernel,
        in_specs=[HBM] * 8,
        out_specs=[VMEM] * 7,
        out_shape=[
            jax.ShapeDtypeStruct((ROWS, W), BF16),
            jax.ShapeDtypeStruct((ROWS, W), BF16),
            jax.ShapeDtypeStruct((LOCAL_COUNT, RHS, W), F32),
            jax.ShapeDtypeStruct((UPPER * RHS, W), F32),
            jax.ShapeDtypeStruct((FLAGS * RHS, W), BF16),
            jax.ShapeDtypeStruct((RHS, W), F32),
            jax.ShapeDtypeStruct((2 * LOCAL_COUNT * RHS, W), F32),
        ],
        scratch_shapes=[
            pltpu.VMEM((4, RHS, W), F32),
            pltpu.VMEM((4, W, W), BF16),
            pltpu.VMEM((1, W, W), BF16),
            pltpu.VMEM((4, 2, W, W), BF16),
            pltpu.VMEM((1, 2, W, W), BF16),
            pltpu.SMEM((1, 4), jnp.int32),
            pltpu.SMEM((1, 4), jnp.int32),
            pltpu.VMEM((1, DEVICES), jnp.int32),
            pltpu.SemaphoreType.DMA((10,)),
        ],
        compiler_params=PARAMS,
    )(
        *[
            pltpu.with_memory_space_constraint(value, pltpu.HBM)
            for value in (rights, linv, uinv, lblk, ublk, widths, far, owner)
        ]
    )


def flag(flags, index):
    return part(flags, index).astype(F32) > 0.5


def choose(test, one, other):
    return jnp.where(test, one.astype(F32), other.astype(F32)).astype(BF16)


def choose_rows(test, one, other, chosen, left):
    wide = jnp.concatenate([test] * 16, axis=0)
    for start in range(0, ROWS, W):
        rows = slice(start, min(start + W, ROWS))
        amount = rows.stop - rows.start
        a, b = (one[rows], other[rows])
        chosen[rows] = choose(wide[:amount], a, b)
        left[rows] = choose(wide[:amount], b, a)


def eliminate(total, low):
    half = total[:RHS].astype(BF16)
    near = times(half, low[:W])
    away = times(half, low[W : 2 * W])
    distance = low[FAR_A : FAR_A + RHS].astype(F32)
    rest = []
    for step in range(1, total.shape[0] // RHS):
        value = part(total, step)
        if step == 1:
            value = value - near
        rest.append(value - jnp.where(distance == float(step), away, 0.0))
    gain = times(half[:, :SHARE], low[GAIN_A:SUMS]).astype(BF16)
    return half, gain, jnp.concatenate(rest, axis=0)


def pass_on(flags, rest, left):
    rows = rest.shape[0]
    wide = jnp.concatenate([flag(flags, ROLE_A)] * (rows // RHS), axis=0)
    left[SUMS : SUMS + rows] = choose(wide, rest.astype(BF16), left[SUMS : SUMS + rows])


def gather_kernel(
    height, own, r2, r1, r3, sums, flags, left, residues, rest, k1, k2, k1q, lp, lq
):
    choose_rows(flag(flags, height - 1), own, r1, k1, lp)
    choose_rows(flag(flags, OTHER_PAIR[height]), r2, r3, k1q, lq)
    choose_rows(flag(flags, height), lp, lq, k2, left)
    rows = slice(SUMS, SUMS + sums.shape[0])
    near = sums[...] + r1[rows].astype(F32)
    other = r2[rows].astype(F32) + r3[rows].astype(F32)
    half_1, gain_1, near = eliminate(near, k1)
    half_1q, gain_1q, other = eliminate(other, k1q)
    half_2, gain_2, value = eliminate(near + other, k2)
    for k, block in enumerate((half_1, gain_1, half_1q, gain_1q, half_2, gain_2)):
        residues[k * RHS : (k + 1) * RHS] = block
    rest[...] = value
    pass_on(flags, value, left)


def gather(height, own, came, sums, flags, both=True):
    message = jax.ShapeDtypeStruct((ROWS, W), BF16)
    kept = 3 if both else 2
    left, residues, rest, *ups = pl.pallas_call(
        functools.partial(gather_kernel, height),
        in_specs=[VMEM] * 6,
        out_specs=[VMEM] * (3 + kept),
        out_shape=[
            message,
            jax.ShapeDtypeStruct((6 * RHS, W), BF16),
            jax.ShapeDtypeStruct((sums.shape[0] - 2 * RHS, W), F32),
        ]
        + [message] * kept,
        scratch_shapes=[pltpu.VMEM((ROWS, W), BF16)] * (5 - kept),
        compiler_params=PARAMS,
    )(own, came[1], came[0], came[2], sums, flags)
    return ups, left, residues, rest


def climb_kernel(height, own, came, sums, flags, chosen, left, residue, rest):
    choose_rows(flag(flags, height - 1), own, came, chosen, left)
    total = sums[...] + came[SUMS : SUMS + sums.shape[0]].astype(F32)
    half, gain, value = eliminate(total, chosen)
    residue[:RHS] = half
    residue[RHS:] = gain
    rest[...] = value
    pass_on(flags, value, left)


def climb(height, own, came, sums, flags):
    message = jax.ShapeDtypeStruct((ROWS, W), BF16)
    return pl.pallas_call(
        functools.partial(climb_kernel, height),
        in_specs=[VMEM] * 4,
        out_specs=[VMEM] * 4,
        out_shape=[
            message,
            message,
            jax.ShapeDtypeStruct((2 * RHS, W), BF16),
            jax.ShapeDtypeStruct((sums.shape[0] - RHS, W), F32),
        ],
        compiler_params=PARAMS,
    )(own, came, sums, flags)


def separator(vectors, index, up, above):
    distance = up[FAR_B : FAR_B + RHS].astype(F32)
    known = jnp.zeros((RHS, W), F32)
    for step, value in enumerate(above, 1):
        known = known + jnp.where(distance == float(step), value.astype(F32), 0.0)
    gain = jnp.concatenate([jnp.zeros((SHARE, W), BF16), up[GAIN_B:FAR_B]], axis=0)
    return (
        part(vectors, 2 * index + 1).astype(F32)
        + times(part(vectors, 2 * index), gain)
        - times(above[0], up[:W])
        - times(known.astype(BF16), up[W : 2 * W])
    ).astype(BF16)


def top_kernel(
    vectors, late, came, mine, flags, u3, u4, u3q, u5, u6, u7, near_out, other_out
):
    wide = jnp.concatenate([flag(flags, UPPER - 1)] * 16, axis=0)
    own = jnp.concatenate([mine[:SHARE], mine[GAIN_B:FAR_B]], axis=0)
    last = choose(wide, own, came[:W])
    residue = part(late, 6).astype(F32) + came[W:].astype(F32)
    above = [times(residue.astype(BF16), last).astype(BF16)]
    for source, index, up in ((late, 2, u7), (late, 0, u6), (vectors, 6, u5), (vectors, 5, u4)):
        above = [separator(source, index, up, above)] + above
    for index, up, out in ((3, u3, near_out), (4, u3q, other_out)):
        out[:RHS] = separator(vectors, index, up, above)
        for step, value in enumerate(above, 1):
            out[step * RHS : (step + 1) * RHS] = value


def top(vectors, late, came, mine, flags, *ups):
    known = jax.ShapeDtypeStruct(((UPPER - LOW) * RHS, W), BF16)
    return pl.pallas_call(
        top_kernel,
        in_specs=[VMEM] * (5 + len(ups)),
        out_specs=[VMEM] * 2,
        out_shape=[known, known],
        compiler_params=PARAMS,
    )(vectors, late, came, mine, flags, *ups)


def select_known(cases, known):
    for test, ref in cases:

        @pl.when(test)
        def _():
            known[...] = ref[...]


def bottom_kernel(vectors, own, a, b, c, u1, u2, u1q, near_out, other_out, known):
    z = lax.axis_index("col") // 4
    first, last = LEADERS
    select_known(
        [
            ((z == (first ^ k)) | (z == (last ^ k)), ref)
            for k, ref in enumerate((own, a, b, c))
        ],
        known,
    )
    above = [part(known, k) for k in range(UPPER - LOW)]
    above = [separator(vectors, 2, u2, above)] + above
    for index, up, out in ((0, u1, near_out), (1, u1q, other_out)):
        out[:RHS] = separator(vectors, index, up, above)
        for step, value in enumerate(above, 1):
            out[step * RHS : (step + 1) * RHS] = value


def bottom(vectors, own, a, b, c, u1, u2, u1q):
    known = jax.ShapeDtypeStruct((UPPER * RHS, W), BF16)
    return pl.pallas_call(
        bottom_kernel,
        in_specs=[VMEM] * 8,
        out_specs=[VMEM] * 2,
        out_shape=[known, known],
        scratch_shapes=[pltpu.VMEM(((UPPER - LOW) * RHS, W), BF16)],
        compiler_params=PARAMS,
    )(vectors, own, a, b, c, u1, u2, u1q)


def descend_kernel(uinv, ublk, slots, level, solved, own, a, b, c, out, known):
    place = (lax.axis_index("col") % 4 + 2 * lax.axis_index("gz")) % 4
    select_known(
        [(place == seated, ref) for seated, ref in enumerate((a, own, b, c))], known
    )
    above = [part(known, k) for k in range(UPPER)]
    own_value = jnp.zeros((RHS, W), F32)
    for k, value in enumerate(above):
        own_value = jnp.where(level[...] == float(k + 1), value.astype(F32), own_value)
    out[0, LOCAL_COUNT] = own_value
    for slot in (2, 1, 0):
        distance = part(slots, LOCAL_COUNT + slot)
        distant = jnp.zeros((RHS, W), F32)
        for step, value in enumerate(above, 1):
            distant = distant + jnp.where(distance == float(step), value.astype(F32), 0.0)
        residue = (
            solved[slot]
            - times_rows(above[0], ublk[0, slot, 0])
            - times_rows(distant.astype(BF16), ublk[0, slot, 1])
        )
        value = jnp.where(
            part(slots, slot) > 0.5, times_rows(residue.astype(BF16), uinv[0, slot]), 0.0
        )
        out[0, slot] = value
        if slot == 2:
            above = [value.astype(BF16)] + above


def descend(uinv, ublk, slots, level, solved, own, a, b, c):
    return pl.pallas_call(
        descend_kernel,
        in_specs=[VMEM] * 9,
        out_specs=VMEM,
        out_shape=jax.ShapeDtypeStruct((1, 4, RHS, W), F32),
        scratch_shapes=[pltpu.VMEM((UPPER * RHS, W), BF16)],
        compiler_params=PARAMS,
    )(uinv, ublk, slots, level, solved, own, a, b, c)


def local(rights, linv, uinv, lblk, ublk, widths, far, owner_level):
    first, second, solved, sums, flags, level, slots = begin(
        rights, linv, uinv, lblk, ublk, widths, far, owner_level.reshape(1, DEVICES)
    )
    r2 = send(first, seats(((2, 0), (3, 1))))
    r1 = send(second, seats(((1, 0), (0, 1))))
    r3 = send(second, seats(((3, 0), (2, 1))))
    came = (r1, r2, r3)
    ups_y, message, residues_y, sums = gather(1, first, came, sums, flags)
    came = [send(message, to_leaders(k)) for k in (1, 2, 3)]
    ups_z, message, residues_z, sums = gather(3, message, came, sums, flags)
    came = send(message, across(4 * (LEADERS[0] ^ LEADERS[1])))
    up_5, message, residue_5, sums = climb(5, message, came, sums, flags)
    came = {k: send(message, across(32 * k)) for k in (2, 1, 3)}
    vectors = jnp.concatenate([residues_y, residues_z, residue_5], axis=0)
    vectors = send(vectors, seats(((0, 1),)))
    came = [came[k] for k in (1, 2, 3)]
    ups_x, message, residues_x, sums = gather(6, message, came, sums, flags, False)
    root = sums.astype(BF16)
    across_came = send(jnp.concatenate([message[:W], root], axis=0), layers(0, 1))
    late = jnp.concatenate([residues_x, root], axis=0)
    late = send(late, seats(((0, 1),)))
    known, known_other = top(
        vectors, late, across_came, message, flags, *ups_z, up_5, *ups_x
    )
    a = send(known, from_leaders(1))
    b = send(known_other, from_leaders(2))
    c = send(known_other, from_leaders(3))
    known, known_other = bottom(vectors, known, a, b, c, *ups_y)
    a = send(known, seats(((1, 0),)))
    b = send(known_other, seats(((1, 2),)))
    c = send(known_other, seats(((1, 3),)))
    return descend(uinv, ublk, slots, level, solved, known, a, b, c)


def solution(mesh):
    split = P(AXES)
    in_specs = (split,) * 7 + (P(),)
    return jax.shard_map(local, mesh=mesh, in_specs=in_specs, out_specs=split, check_vma=False)
```

```python
import functools

import jax
import jax.numpy as jnp
from jax import lax
from jax.experimental import pallas as pl
from jax.experimental.pallas import tpu as pltpu
from jax.sharding import PartitionSpec as P

W = 256
RHS = 16
LOCAL_COUNT = 3
UPPER = 8
LOW = 2
DEVICES = 256
AXES = ("gz", "row", "col")
BF16 = jnp.bfloat16
F32 = jnp.float32
SHARE = 64
FAR_A = 2 * W
GAIN_A = FAR_A + RHS
SUMS = GAIN_A + SHARE
GAIN_B = 2 * W
ROWS = GAIN_B + W - SHARE
ROWS_Y = SUMS + UPPER * RHS
GATHERS = (1, 3, 6)
ORDER = {1: (2, 1, 3), 3: (2, 1, 3), 6: (1, 2, 3)}
OTHER_PAIR = {low: UPPER + k for k, low in enumerate(GATHERS)}
ROLE_A = UPPER + len(GATHERS)
FLAGS = ROLE_A + 1
LEADERS = (2, 5)
VMEM = pl.BlockSpec(memory_space=pltpu.VMEM)
HBM = pl.BlockSpec(memory_space=pltpu.HBM)
PARAMS = pltpu.CompilerParams(vmem_limit_bytes=24 * 1024 * 1024)


def seat(t):
    return (t % 4 - (0 if t < DEVICES // 2 else 2)) % 4


def at_seat(t, place):
    return t - t % 4 + (place + (0 if t < DEVICES // 2 else 2)) % 4


def send(value, pairs):
    return lax.ppermute(value, AXES, pairs)


def seats(moves):
    firsts = [t for t in range(DEVICES) if t % 4 == 0]
    return [(at_seat(t, a), at_seat(t, b)) for t in firsts for a, b in moves]


def leads(t):
    return seat(t) < 2 and t // 4 % 8 in LEADERS


def to_leaders(distance):
    return [(t ^ (4 * distance), t) for t in range(DEVICES) if leads(t)]


def from_leaders(distance):
    return [(t, t ^ (4 * distance)) for t in range(DEVICES) if leads(t) and seat(t) == 1]


def across(mask):
    return [(t, t ^ mask) for t in range(DEVICES) if leads(t)]


def layers(a, b):
    firsts = [t for t in range(DEVICES) if t % 4 == 0 and t // 4 % 8 in LEADERS]
    return [(at_seat(t, a), at_seat(t ^ (DEVICES // 2), b)) for t in firsts]


def times(vectors, blocks):
    return jnp.dot(vectors, blocks, preferred_element_type=F32)


def times_rows(vectors, blocks):
    return lax.dot_general(
        vectors, blocks, (((1,), (1,)), ((), ())), preferred_element_type=F32
    )


def row_pad(width):
    return lax.broadcasted_iota(jnp.int32, (1, W), 1) < width


def part(rows, index):
    return rows[index * RHS : (index + 1) * RHS]


def begin_kernel(
    rights_in,
    linv_in,
    uinv_in,
    lblk_in,
    ublk_in,
    widths_in,
    far_in,
    owner_in,
    first,
    second,
    solved,
    sums,
    flags,
    level,
    slots,
    rights,
    linv,
    uinv,
    lblk,
    ublk,
    widths,
    far,
    owner,
    sems,
):
    own = pl.ds(LOCAL_COUNT, 1)
    rest = pl.ds(0, LOCAL_COUNT)
    small = [
        pltpu.make_async_copy(widths_in, widths, sems.at[0]),
        pltpu.make_async_copy(far_in, far, sems.at[1]),
    ]
    owner_copy = pltpu.make_async_copy(owner_in, owner, sems.at[9])
    owner_copy.start()
    mine = [
        pltpu.make_async_copy(linv_in.at[0, own], linv.at[own], sems.at[2]),
        pltpu.make_async_copy(lblk_in.at[0, own], lblk.at[own], sems.at[3]),
        pltpu.make_async_copy(uinv_in.at[0, own], uinv, sems.at[4]),
        pltpu.make_async_copy(ublk_in.at[0, own], ublk, sems.at[5]),
    ]
    leaf = [
        pltpu.make_async_copy(rights_in.at[0], rights, sems.at[6]),
        pltpu.make_async_copy(linv_in.at[0, rest], linv.at[rest], sems.at[7]),
        pltpu.make_async_copy(lblk_in.at[0, rest], lblk.at[rest], sems.at[8]),
    ]
    for copy in small + mine + leaf:
        copy.start()
    gz = lax.axis_index("gz")
    col = lax.axis_index("col")
    me = gz * (DEVICES // 2) + lax.axis_index("row") * (DEVICES // 8) + col
    y = col % 4
    place = (y + 2 * gz) % 4
    everyone = lax.broadcasted_iota(jnp.int32, (1, DEVICES), 1)
    owner_copy.wait()
    owners = owner[...]

    def spread(value):
        return jnp.broadcast_to(value, (RHS, W))

    def found(chosen):
        return spread(jnp.max(jnp.where(chosen, 1.0, 0.0), axis=1, keepdims=True))

    for v in range(1, UPPER + 1):
        half = lax.shift_right_logical(everyone, v - 1) == lax.shift_right_logical(me, v - 1)
        flags[(v - 1) * RHS : v * RHS] = found(half & (owners == v)).astype(BF16)
    for v in GATHERS:
        half = lax.shift_right_logical(everyone, v - 1) == (
            lax.shift_right_logical(me, v - 1) ^ 2
        )
        flags[OTHER_PAIR[v] * RHS : (OTHER_PAIR[v] + 1) * RHS] = found(
            half & (owners == v)
        ).astype(BF16)
    flags[ROLE_A * RHS : (ROLE_A + 1) * RHS] = jnp.full(
        (RHS, W), jnp.where(place == 0, 1.0, 0.0), F32
    ).astype(BF16)
    my_level = spread(
        jnp.sum(jnp.where(everyone == me, owners, 0).astype(F32), axis=1, keepdims=True)
    )
    level[...] = my_level
    for copy in small + mine:
        copy.wait()
    pad = lax.broadcasted_iota(jnp.int32, (W, 1), 0) < widths[0, LOCAL_COUNT]
    distance = jnp.full((RHS, W), far[0, LOCAL_COUNT], jnp.int32).astype(F32).astype(BF16)
    lower = jnp.where(pad, linv[LOCAL_COUNT].astype(F32), 0.0).astype(BF16)
    upper = jnp.where(pad, uinv[0].astype(F32), 0.0).astype(BF16)
    low_blocks = [times(lblk[LOCAL_COUNT, b], lower).T.astype(BF16) for b in range(2)]
    up_blocks = [times(upper, ublk[0, b]).T.astype(BF16) for b in range(2)]
    up_blocks.append(times(upper, lower).T.astype(BF16))
    for copy in leaf:
        copy.wait()
    for v in range(1, UPPER + 1):
        sums[(v - 1) * RHS : v * RHS] = jnp.where(my_level == v, rights[LOCAL_COUNT], 0.0)
    pending = jnp.zeros((RHS, W), F32)
    for slot in range(LOCAL_COUNT):
        residue = rights[slot]
        if slot == LOCAL_COUNT - 1:
            residue = residue - pending
        inside = jnp.broadcast_to(row_pad(widths[0, slot]), (RHS, W))
        forward = jnp.where(inside, times_rows(residue.astype(BF16), linv[slot]), 0.0)
        solved[slot] = forward
        slots[slot * RHS : (slot + 1) * RHS] = jnp.where(inside, 1.0, 0.0)
        slots[(LOCAL_COUNT + slot) * RHS : (LOCAL_COUNT + slot + 1) * RHS] = jnp.full(
            (RHS, W), far[0, slot], jnp.int32
        ).astype(F32)
        half = forward.astype(BF16)
        near = times_rows(half, lblk[slot, 0])
        away = times_rows(half, lblk[slot, 1])
        if slot == LOCAL_COUNT - 1:
            sums[:RHS] = sums[:RHS] - near
            target = far[0, slot]
        else:
            pending = pending + near
            target = far[0, slot] - 1
        for v in range(1, UPPER + 1):
            rows = slice((v - 1) * RHS, v * RHS)
            sums[rows] = sums[rows] - jnp.where(target == v, away, 0.0)
    halves = sums[...].astype(BF16)

    def write(low, up):
        wide = jnp.concatenate([my_level] * (W // RHS), axis=0) == float(UPPER)
        low[:W] = choose(wide, up_blocks[2], low_blocks[0])
        low[W : 2 * W] = low_blocks[1]
        low[FAR_A:GAIN_A] = distance
        low[GAIN_A:SUMS] = up_blocks[2][:SHARE]
        low[SUMS:] = halves
        up[:SHARE] = choose(wide[:SHARE], up_blocks[2][:SHARE], up_blocks[0][:SHARE])
        up[SHARE:W] = up_blocks[0][SHARE:]
        up[W : 2 * W] = up_blocks[1]
        up[GAIN_B:ROWS] = up_blocks[2][SHARE:]
        up[ROWS:] = jnp.zeros((ROWS_Y - ROWS, W), BF16)

    @pl.when(place % 2 == 0)
    def _():
        write(first, second)

    @pl.when(place % 2 == 1)
    def _():
        write(second, first)


def begin(rights, linv, uinv, lblk, ublk, widths, far, owner):
    return pl.pallas_call(
        begin_kernel,
        in_specs=[HBM] * 8,
        out_specs=[VMEM] * 7,
        out_shape=[
            jax.ShapeDtypeStruct((ROWS_Y, W), BF16),
            jax.ShapeDtypeStruct((ROWS_Y, W), BF16),
            jax.ShapeDtypeStruct((LOCAL_COUNT, RHS, W), F32),
            jax.ShapeDtypeStruct((UPPER * RHS, W), F32),
            jax.ShapeDtypeStruct((FLAGS * RHS, W), BF16),
            jax.ShapeDtypeStruct((RHS, W), F32),
            jax.ShapeDtypeStruct((2 * LOCAL_COUNT * RHS, W), F32),
        ],
        scratch_shapes=[
            pltpu.VMEM((4, RHS, W), F32),
            pltpu.VMEM((4, W, W), BF16),
            pltpu.VMEM((1, W, W), BF16),
            pltpu.VMEM((4, 2, W, W), BF16),
            pltpu.VMEM((1, 2, W, W), BF16),
            pltpu.SMEM((1, 4), jnp.int32),
            pltpu.SMEM((1, 4), jnp.int32),
            pltpu.VMEM((1, DEVICES), jnp.int32),
            pltpu.SemaphoreType.DMA((10,)),
        ],
        compiler_params=PARAMS,
    )(
        *[
            pltpu.with_memory_space_constraint(value, pltpu.HBM)
            for value in (rights, linv, uinv, lblk, ublk, widths, far, owner)
        ]
    )


def flag(flags, index):
    return part(flags, index).astype(F32) > 0.5


def choose(test, one, other):
    return jnp.where(test, one.astype(F32), other.astype(F32)).astype(BF16)


def choose_rows(test, one, other, chosen, left):
    wide = jnp.concatenate([test] * 16, axis=0)
    for start in range(0, ROWS, W):
        rows = slice(start, min(start + W, ROWS))
        amount = rows.stop - rows.start
        a, b = (one[rows], other[rows])
        chosen[rows] = choose(wide[:amount], a, b)
        left[rows] = choose(wide[:amount], b, a)


def eliminate(total, low):
    half = total[:RHS].astype(BF16)
    near = times(half, low[:W])
    away = times(half, low[W : 2 * W])
    distance = low[FAR_A : FAR_A + RHS].astype(F32)
    rest = []
    for step in range(1, total.shape[0] // RHS):
        value = part(total, step)
        if step == 1:
            value = value - near
        rest.append(value - jnp.where(distance == float(step), away, 0.0))
    gain = times(half[:, :SHARE], low[GAIN_A:SUMS]).astype(BF16)
    return half, gain, jnp.concatenate(rest, axis=0)


def pass_on(flags, rest, left):
    rows = rest.shape[0]
    wide = jnp.concatenate([flag(flags, ROLE_A)] * (rows // RHS), axis=0)
    left[SUMS : SUMS + rows] = choose(wide, rest.astype(BF16), left[SUMS : SUMS + rows])


def gather_kernel(
    height, own, a, b, c, sums, flags, left, residues, rest, k1, k2, k1q, lp, lq
):
    r1, r2, r3 = (dict(zip(ORDER[height], (a, b, c)))[k] for k in (1, 2, 3))
    choose_rows(flag(flags, height - 1), own, r1, k1, lp)
    choose_rows(flag(flags, OTHER_PAIR[height]), r2, r3, k1q, lq)
    choose_rows(flag(flags, height), lp, lq, k2, left)
    rows = slice(SUMS, SUMS + sums.shape[0])
    near = sums[...] + r1[rows].astype(F32)
    other = r2[rows].astype(F32) + r3[rows].astype(F32)
    half_1, gain_1, near = eliminate(near, k1)
    half_1q, gain_1q, other = eliminate(other, k1q)
    half_2, gain_2, value = eliminate(near + other, k2)
    for k, block in enumerate((half_1, gain_1, half_1q, gain_1q, half_2, gain_2)):
        residues[k * RHS : (k + 1) * RHS] = block
    row = lax.broadcasted_iota(jnp.int32, (RHS, W), 0)
    far_1, far_1q, far_2 = (k[FAR_A:GAIN_A].astype(F32) for k in (k1, k1q, k2))
    residues[6 * RHS :] = jnp.where(
        row == 0, far_1, jnp.where(row == 1, far_1q, far_2)
    ).astype(BF16)
    rest[...] = value
    pass_on(flags, value, left)


def gather(height, own, came, sums, flags, both=True):
    message = jax.ShapeDtypeStruct((ROWS, W), BF16)
    kept = 3 if both else 2
    left, residues, rest, *ups = pl.pallas_call(
        functools.partial(gather_kernel, height),
        in_specs=[VMEM] * 6,
        out_specs=[VMEM] * (3 + kept),
        out_shape=[
            message,
            jax.ShapeDtypeStruct((7 * RHS, W), BF16),
            jax.ShapeDtypeStruct((sums.shape[0] - 2 * RHS, W), F32),
        ]
        + [message] * kept,
        scratch_shapes=[pltpu.VMEM((ROWS, W), BF16)] * (5 - kept),
        compiler_params=PARAMS,
    )(own, *[came[k - 1] for k in ORDER[height]], sums, flags)
    return ups, left, residues, rest


def climb_kernel(height, own, came, sums, flags, chosen, left, residue, rest):
    choose_rows(flag(flags, height - 1), own, came, chosen, left)
    total = sums[...] + came[SUMS : SUMS + sums.shape[0]].astype(F32)
    half, gain, value = eliminate(total, chosen)
    residue[:RHS] = half
    residue[RHS : 2 * RHS] = gain
    residue[2 * RHS :] = chosen[FAR_A:GAIN_A]
    rest[...] = value
    pass_on(flags, value, left)


def climb(height, own, came, sums, flags):
    message = jax.ShapeDtypeStruct((ROWS, W), BF16)
    return pl.pallas_call(
        functools.partial(climb_kernel, height),
        in_specs=[VMEM] * 4,
        out_specs=[VMEM] * 4,
        out_shape=[
            message,
            message,
            jax.ShapeDtypeStruct((3 * RHS, W), BF16),
            jax.ShapeDtypeStruct((sums.shape[0] - RHS, W), F32),
        ],
        compiler_params=PARAMS,
    )(own, came, sums, flags)


def separator(vectors, place, up, above):
    start, distances, index = place
    distance = part(vectors, distances).astype(F32)[index : index + 1]
    known = jnp.zeros((RHS, W), F32)
    for step, value in enumerate(above, 1):
        known = known + jnp.where(distance == float(step), value.astype(F32), 0.0)
    gain = jnp.concatenate([jnp.zeros((SHARE, W), BF16), up[GAIN_B:ROWS]], axis=0)
    return (
        part(vectors, start + 2 * index + 1).astype(F32)
        + times(part(vectors, start + 2 * index), gain)
        - times(above[0], up[:W])
        - times(known.astype(BF16), up[W : 2 * W])
    ).astype(BF16)


def top_kernel(
    vectors, late, came, mine, flags, u3, u4, u3q, u5, u6, u7, near_out, other_out
):
    wide = jnp.concatenate([flag(flags, UPPER - 1)] * 16, axis=0)
    own = jnp.concatenate([mine[:SHARE], mine[GAIN_B:ROWS]], axis=0)
    last = choose(wide, own, came[:W])
    residue = part(late, 7).astype(F32) + came[W:].astype(F32)
    above = [times(residue.astype(BF16), last).astype(BF16)]
    for source, index, up in (
        (late, (0, 6, 2), u7),
        (late, (0, 6, 0), u6),
        (vectors, (14, 16, 0), u5),
        (vectors, (7, 13, 2), u4),
    ):
        above = [separator(source, index, up, above)] + above
    for index, up, out in (((7, 13, 0), u3, near_out), ((7, 13, 1), u3q, other_out)):
        out[:RHS] = separator(vectors, index, up, above)
        for step, value in enumerate(above, 1):
            out[step * RHS : (step + 1) * RHS] = value


def top(vectors, late, came, mine, flags, *ups):
    known = jax.ShapeDtypeStruct(((UPPER - LOW) * RHS, W), BF16)
    return pl.pallas_call(
        top_kernel,
        in_specs=[VMEM] * (5 + len(ups)),
        out_specs=[VMEM] * 2,
        out_shape=[known, known],
        compiler_params=PARAMS,
    )(vectors, late, came, mine, flags, *ups)


def select_known(cases, known):
    for test, ref in cases:

        @pl.when(test)
        def _():
            known[...] = ref[...]


def bottom_kernel(vectors, own, a, b, c, u1, u2, u1q, near_out, other_out, known):
    z = lax.axis_index("col") // 4
    first, last = LEADERS
    select_known(
        [
            ((z == (first ^ k)) | (z == (last ^ k)), ref)
            for k, ref in enumerate((own, a, b, c))
        ],
        known,
    )
    above = [part(known, k) for k in range(UPPER - LOW)]
    above = [separator(vectors, (0, 6, 2), u2, above)] + above
    for index, up, out in (((0, 6, 0), u1, near_out), ((0, 6, 1), u1q, other_out)):
        out[:RHS] = separator(vectors, index, up, above)
        for step, value in enumerate(above, 1):
            out[step * RHS : (step + 1) * RHS] = value


def bottom(vectors, own, a, b, c, u1, u2, u1q):
    known = jax.ShapeDtypeStruct((UPPER * RHS, W), BF16)
    return pl.pallas_call(
        bottom_kernel,
        in_specs=[VMEM] * 8,
        out_specs=[VMEM] * 2,
        out_shape=[known, known],
        scratch_shapes=[pltpu.VMEM(((UPPER - LOW) * RHS, W), BF16)],
        compiler_params=PARAMS,
    )(vectors, own, a, b, c, u1, u2, u1q)


def descend_kernel(uinv, ublk, slots, level, solved, own, a, b, c, out, known):
    place = (lax.axis_index("col") % 4 + 2 * lax.axis_index("gz")) % 4
    select_known(
        [(place == seated, ref) for seated, ref in enumerate((a, own, b, c))], known
    )
    above = [part(known, k) for k in range(UPPER)]
    own_value = jnp.zeros((RHS, W), F32)
    for k, value in enumerate(above):
        own_value = jnp.where(level[...] == float(k + 1), value.astype(F32), own_value)
    out[0, LOCAL_COUNT] = own_value
    for slot in (2, 1, 0):
        distance = part(slots, LOCAL_COUNT + slot)
        distant = jnp.zeros((RHS, W), F32)
        for step, value in enumerate(above, 1):
            distant = distant + jnp.where(distance == float(step), value.astype(F32), 0.0)
        residue = (
            solved[slot]
            - times_rows(above[0], ublk[0, slot, 0])
            - times_rows(distant.astype(BF16), ublk[0, slot, 1])
        )
        value = jnp.where(
            part(slots, slot) > 0.5, times_rows(residue.astype(BF16), uinv[0, slot]), 0.0
        )
        out[0, slot] = value
        if slot == 2:
            above = [value.astype(BF16)] + above


def descend(uinv, ublk, slots, level, solved, own, a, b, c):
    return pl.pallas_call(
        descend_kernel,
        in_specs=[VMEM] * 9,
        out_specs=VMEM,
        out_shape=jax.ShapeDtypeStruct((1, 4, RHS, W), F32),
        scratch_shapes=[pltpu.VMEM((UPPER * RHS, W), BF16)],
        compiler_params=PARAMS,
    )(uinv, ublk, slots, level, solved, own, a, b, c)


def local(rights, linv, uinv, lblk, ublk, widths, far, owner_level):
    first, second, solved, sums, flags, level, slots = begin(
        rights, linv, uinv, lblk, ublk, widths, far, owner_level.reshape(1, DEVICES)
    )
    r2 = send(first, seats(((2, 0), (3, 1))))
    r1 = send(second, seats(((1, 0), (0, 1))))
    r3 = send(second, seats(((3, 0), (2, 1))))
    came = (r1, r2, r3)
    ups_y, message, residues_y, sums = gather(1, first, came, sums, flags)
    came = [send(message, to_leaders(k)) for k in (1, 2, 3)]
    ups_z, message, residues_z, sums = gather(3, message, came, sums, flags)
    came = send(message, across(4 * (LEADERS[0] ^ LEADERS[1])))
    up_5, message, residue_5, sums = climb(5, message, came, sums, flags)
    came = {k: send(message, across(32 * k)) for k in (2, 1, 3)}
    vectors = jnp.concatenate([residues_y, residues_z, residue_5], axis=0)
    vectors = send(vectors, seats(((0, 1),)))
    came = [came[k] for k in (1, 2, 3)]
    ups_x, message, residues_x, sums = gather(6, message, came, sums, flags, False)
    root = sums.astype(BF16)
    across_came = send(jnp.concatenate([message[:W], root], axis=0), layers(0, 1))
    late = jnp.concatenate([residues_x, root], axis=0)
    late = send(late, seats(((0, 1),)))
    known, known_other = top(
        vectors, late, across_came, message, flags, *ups_z, up_5, *ups_x
    )
    a = send(known, from_leaders(1))
    b = send(known_other, from_leaders(2))
    c = send(known_other, from_leaders(3))
    known, known_other = bottom(vectors, known, a, b, c, *ups_y)
    a = send(known, seats(((1, 0),)))
    b = send(known_other, seats(((1, 2),)))
    c = send(known_other, seats(((1, 3),)))
    return descend(uinv, ublk, slots, level, solved, known, a, b, c)


def solution(mesh):
    split = P(AXES)
    in_specs = (split,) * 7 + (P(),)
    return jax.shard_map(local, mesh=mesh, in_specs=in_specs, out_specs=split, check_vma=False)
```

```python
import functools

import jax
import jax.numpy as jnp
from jax import lax
from jax.experimental import pallas as pl
from jax.experimental.pallas import tpu as pltpu
from jax.sharding import PartitionSpec as P

W = 256
RHS = 16
LOCAL_COUNT = 3
UPPER = 8
LOW = 2
DEVICES = 256
AXES = ("gz", "row", "col")
BF16 = jnp.bfloat16
F32 = jnp.float32
SHARE = 64
FAR_A = 2 * W
GAIN_A = FAR_A + RHS
SUMS = GAIN_A + SHARE
GAIN_B = 2 * W
ROWS = GAIN_B + W - SHARE
ROWS_Y = SUMS + UPPER * RHS
GATHERS = (1, 3, 6)
ORDER = {1: (2, 1, 3), 3: (2, 1, 3), 6: (1, 2, 3)}
OTHER_PAIR = {low: UPPER + k for k, low in enumerate(GATHERS)}
ROLE_A = UPPER + len(GATHERS)
FLAGS = ROLE_A + 1
LEADERS = (2, 5)
VMEM = pl.BlockSpec(memory_space=pltpu.VMEM)
HBM = pl.BlockSpec(memory_space=pltpu.HBM)
PARAMS = pltpu.CompilerParams(vmem_limit_bytes=24 * 1024 * 1024)


def seat(t):
    return (t % 4 - (0 if t < DEVICES // 2 else 2)) % 4


def at_seat(t, place):
    return t - t % 4 + (place + (0 if t < DEVICES // 2 else 2)) % 4


def send(value, pairs):
    return lax.ppermute(value, AXES, pairs)


def seats(moves):
    firsts = [t for t in range(DEVICES) if t % 4 == 0]
    return [(at_seat(t, a), at_seat(t, b)) for t in firsts for a, b in moves]


def leads(t):
    return seat(t) < 2 and t // 4 % 8 in LEADERS


def to_leaders(distance):
    return [(t ^ (4 * distance), t) for t in range(DEVICES) if leads(t)]


def from_leaders(distance):
    return [(t, t ^ (4 * distance)) for t in range(DEVICES) if leads(t) and seat(t) == 1]


def across(mask):
    return [(t, t ^ mask) for t in range(DEVICES) if leads(t)]


def layers(a, b):
    firsts = [t for t in range(DEVICES) if t % 4 == 0 and t // 4 % 8 in LEADERS]
    return [(at_seat(t, a), at_seat(t ^ (DEVICES // 2), b)) for t in firsts]


def times(vectors, blocks):
    return jnp.dot(vectors, blocks, preferred_element_type=F32)


def times_rows(vectors, blocks):
    return lax.dot_general(
        vectors, blocks, (((1,), (1,)), ((), ())), preferred_element_type=F32
    )


def row_pad(width):
    return lax.broadcasted_iota(jnp.int32, (1, W), 1) < width


def part(rows, index):
    return rows[index * RHS : (index + 1) * RHS]


def begin_kernel(
    rights_in,
    linv_in,
    uinv_in,
    lblk_in,
    ublk_in,
    widths_in,
    far_in,
    owner_in,
    first,
    second,
    solved,
    sums,
    flags,
    level,
    slots,
    rights,
    linv,
    uinv,
    lblk,
    ublk,
    widths,
    far,
    owner,
    sems,
):
    own = pl.ds(LOCAL_COUNT, 1)
    rest = pl.ds(0, LOCAL_COUNT)
    small = [
        pltpu.make_async_copy(widths_in, widths, sems.at[0]),
        pltpu.make_async_copy(far_in, far, sems.at[1]),
    ]
    owner_copy = pltpu.make_async_copy(owner_in, owner, sems.at[9])
    owner_copy.start()
    mine = [
        pltpu.make_async_copy(linv_in.at[0, own], linv.at[own], sems.at[2]),
        pltpu.make_async_copy(lblk_in.at[0, own], lblk.at[own], sems.at[3]),
        pltpu.make_async_copy(uinv_in.at[0, own], uinv, sems.at[4]),
        pltpu.make_async_copy(ublk_in.at[0, own], ublk, sems.at[5]),
    ]
    leaf = [
        pltpu.make_async_copy(rights_in.at[0], rights, sems.at[6]),
        pltpu.make_async_copy(linv_in.at[0, rest], linv.at[rest], sems.at[7]),
        pltpu.make_async_copy(lblk_in.at[0, rest], lblk.at[rest], sems.at[8]),
    ]
    for copy in small + mine + leaf:
        copy.start()
    gz = lax.axis_index("gz")
    col = lax.axis_index("col")
    me = gz * (DEVICES // 2) + lax.axis_index("row") * (DEVICES // 8) + col
    y = col % 4
    place = (y + 2 * gz) % 4
    everyone = lax.broadcasted_iota(jnp.int32, (1, DEVICES), 1)
    owner_copy.wait()
    owners = owner[...]

    def spread(value):
        return jnp.broadcast_to(value, (RHS, W))

    def found(chosen):
        return spread(jnp.max(jnp.where(chosen, 1.0, 0.0), axis=1, keepdims=True))

    for v in range(1, UPPER + 1):
        half = lax.shift_right_logical(everyone, v - 1) == lax.shift_right_logical(me, v - 1)
        flags[(v - 1) * RHS : v * RHS] = found(half & (owners == v)).astype(BF16)
    for v in GATHERS:
        half = lax.shift_right_logical(everyone, v - 1) == (
            lax.shift_right_logical(me, v - 1) ^ 2
        )
        flags[OTHER_PAIR[v] * RHS : (OTHER_PAIR[v] + 1) * RHS] = found(
            half & (owners == v)
        ).astype(BF16)
    flags[ROLE_A * RHS : (ROLE_A + 1) * RHS] = jnp.full(
        (RHS, W), jnp.where(place == 0, 1.0, 0.0), F32
    ).astype(BF16)
    my_level = spread(
        jnp.sum(jnp.where(everyone == me, owners, 0).astype(F32), axis=1, keepdims=True)
    )
    level[...] = my_level
    for copy in small + mine:
        copy.wait()
    pad = lax.broadcasted_iota(jnp.int32, (W, 1), 0) < widths[0, LOCAL_COUNT]
    distance = jnp.full((RHS, W), far[0, LOCAL_COUNT], jnp.int32).astype(F32).astype(BF16)
    lower = jnp.where(pad, linv[LOCAL_COUNT].astype(F32), 0.0).astype(BF16)
    upper = jnp.where(pad, uinv[0].astype(F32), 0.0).astype(BF16)
    turned = lower.T
    low_blocks = [times_rows(turned, lblk[LOCAL_COUNT, b]).astype(BF16) for b in range(2)]
    up_blocks = [times_rows(ublk[0, b].T, upper).astype(BF16) for b in range(2)]
    up_blocks.append(times_rows(turned, upper).astype(BF16))
    for copy in leaf:
        copy.wait()
    for v in range(1, UPPER + 1):
        sums[(v - 1) * RHS : v * RHS] = jnp.where(my_level == v, rights[LOCAL_COUNT], 0.0)
    pending = jnp.zeros((RHS, W), F32)
    for slot in range(LOCAL_COUNT):
        residue = rights[slot]
        if slot == LOCAL_COUNT - 1:
            residue = residue - pending
        inside = jnp.broadcast_to(row_pad(widths[0, slot]), (RHS, W))
        forward = jnp.where(inside, times_rows(residue.astype(BF16), linv[slot]), 0.0)
        solved[slot] = forward
        slots[slot * RHS : (slot + 1) * RHS] = jnp.where(inside, 1.0, 0.0)
        slots[(LOCAL_COUNT + slot) * RHS : (LOCAL_COUNT + slot + 1) * RHS] = jnp.full(
            (RHS, W), far[0, slot], jnp.int32
        ).astype(F32)
        half = forward.astype(BF16)
        near = times_rows(half, lblk[slot, 0])
        away = times_rows(half, lblk[slot, 1])
        if slot == LOCAL_COUNT - 1:
            sums[:RHS] = sums[:RHS] - near
            target = far[0, slot]
        else:
            pending = pending + near
            target = far[0, slot] - 1
        for v in range(1, UPPER + 1):
            rows = slice((v - 1) * RHS, v * RHS)
            sums[rows] = sums[rows] - jnp.where(target == v, away, 0.0)
    halves = sums[...].astype(BF16)

    def write(low, up):
        wide = jnp.concatenate([my_level] * (W // RHS), axis=0) == float(UPPER)
        low[:W] = choose(wide, up_blocks[2], low_blocks[0])
        low[W : 2 * W] = low_blocks[1]
        low[FAR_A:GAIN_A] = distance
        low[GAIN_A:SUMS] = up_blocks[2][:SHARE]
        low[SUMS:] = halves
        up[:SHARE] = choose(wide[:SHARE], up_blocks[2][:SHARE], up_blocks[0][:SHARE])
        up[SHARE:W] = up_blocks[0][SHARE:]
        up[W : 2 * W] = up_blocks[1]
        up[GAIN_B:ROWS] = up_blocks[2][SHARE:]
        up[ROWS:] = jnp.zeros((ROWS_Y - ROWS, W), BF16)

    @pl.when(place % 2 == 0)
    def _():
        write(first, second)

    @pl.when(place % 2 == 1)
    def _():
        write(second, first)


def begin(rights, linv, uinv, lblk, ublk, widths, far, owner):
    return pl.pallas_call(
        begin_kernel,
        in_specs=[HBM] * 8,
        out_specs=[VMEM] * 7,
        out_shape=[
            jax.ShapeDtypeStruct((ROWS_Y, W), BF16),
            jax.ShapeDtypeStruct((ROWS_Y, W), BF16),
            jax.ShapeDtypeStruct((LOCAL_COUNT, RHS, W), F32),
            jax.ShapeDtypeStruct((UPPER * RHS, W), F32),
            jax.ShapeDtypeStruct((FLAGS * RHS, W), BF16),
            jax.ShapeDtypeStruct((RHS, W), F32),
            jax.ShapeDtypeStruct((2 * LOCAL_COUNT * RHS, W), F32),
        ],
        scratch_shapes=[
            pltpu.VMEM((4, RHS, W), F32),
            pltpu.VMEM((4, W, W), BF16),
            pltpu.VMEM((1, W, W), BF16),
            pltpu.VMEM((4, 2, W, W), BF16),
            pltpu.VMEM((1, 2, W, W), BF16),
            pltpu.SMEM((1, 4), jnp.int32),
            pltpu.SMEM((1, 4), jnp.int32),
            pltpu.VMEM((1, DEVICES), jnp.int32),
            pltpu.SemaphoreType.DMA((10,)),
        ],
        compiler_params=PARAMS,
    )(
        *[
            pltpu.with_memory_space_constraint(value, pltpu.HBM)
            for value in (rights, linv, uinv, lblk, ublk, widths, far, owner)
        ]
    )


def flag(flags, index):
    return part(flags, index).astype(F32) > 0.5


def choose(test, one, other):
    return jnp.where(test, one.astype(F32), other.astype(F32)).astype(BF16)


def choose_rows(test, one, other, chosen, left):
    wide = jnp.concatenate([test] * 16, axis=0)
    for start in range(0, ROWS, W):
        rows = slice(start, min(start + W, ROWS))
        amount = rows.stop - rows.start
        a, b = (one[rows], other[rows])
        chosen[rows] = choose(wide[:amount], a, b)
        left[rows] = choose(wide[:amount], b, a)


def eliminate(total, low):
    half = total[:RHS].astype(BF16)
    near = times(half, low[:W])
    away = times(half, low[W : 2 * W])
    distance = low[FAR_A : FAR_A + RHS].astype(F32)
    rest = []
    for step in range(1, total.shape[0] // RHS):
        value = part(total, step)
        if step == 1:
            value = value - near
        rest.append(value - jnp.where(distance == float(step), away, 0.0))
    gain = times(half[:, :SHARE], low[GAIN_A:SUMS]).astype(BF16)
    return half, gain, jnp.concatenate(rest, axis=0)


def pass_on(flags, rest, left):
    rows = rest.shape[0]
    wide = jnp.concatenate([flag(flags, ROLE_A)] * (rows // RHS), axis=0)
    left[SUMS : SUMS + rows] = choose(wide, rest.astype(BF16), left[SUMS : SUMS + rows])


def gather_kernel(
    height, own, a, b, c, sums, flags, left, residues, rest, k1, k2, k1q, lp, lq
):
    r1, r2, r3 = (dict(zip(ORDER[height], (a, b, c)))[k] for k in (1, 2, 3))
    choose_rows(flag(flags, height - 1), own, r1, k1, lp)
    choose_rows(flag(flags, OTHER_PAIR[height]), r2, r3, k1q, lq)
    choose_rows(flag(flags, height), lp, lq, k2, left)
    rows = slice(SUMS, SUMS + sums.shape[0])
    near = sums[...] + r1[rows].astype(F32)
    other = r2[rows].astype(F32) + r3[rows].astype(F32)
    half_1, gain_1, near = eliminate(near, k1)
    half_1q, gain_1q, other = eliminate(other, k1q)
    half_2, gain_2, value = eliminate(near + other, k2)
    for k, block in enumerate((half_1, gain_1, half_1q, gain_1q, half_2, gain_2)):
        residues[k * RHS : (k + 1) * RHS] = block
    row = lax.broadcasted_iota(jnp.int32, (RHS, W), 0)
    far_1, far_1q, far_2 = (k[FAR_A:GAIN_A].astype(F32) for k in (k1, k1q, k2))
    residues[6 * RHS :] = jnp.where(
        row == 0, far_1, jnp.where(row == 1, far_1q, far_2)
    ).astype(BF16)
    rest[...] = value
    pass_on(flags, value, left)


def gather(height, own, came, sums, flags, both=True):
    message = jax.ShapeDtypeStruct((ROWS, W), BF16)
    kept = 3 if both else 2
    left, residues, rest, *ups = pl.pallas_call(
        functools.partial(gather_kernel, height),
        in_specs=[VMEM] * 6,
        out_specs=[VMEM] * (3 + kept),
        out_shape=[
            message,
            jax.ShapeDtypeStruct((7 * RHS, W), BF16),
            jax.ShapeDtypeStruct((sums.shape[0] - 2 * RHS, W), F32),
        ]
        + [message] * kept,
        scratch_shapes=[pltpu.VMEM((ROWS, W), BF16)] * (5 - kept),
        compiler_params=PARAMS,
    )(own, *[came[k - 1] for k in ORDER[height]], sums, flags)
    return ups, left, residues, rest


def climb_kernel(height, own, came, sums, flags, chosen, left, residue, rest):
    choose_rows(flag(flags, height - 1), own, came, chosen, left)
    total = sums[...] + came[SUMS : SUMS + sums.shape[0]].astype(F32)
    half, gain, value = eliminate(total, chosen)
    residue[:RHS] = half
    residue[RHS : 2 * RHS] = gain
    residue[2 * RHS :] = chosen[FAR_A:GAIN_A]
    rest[...] = value
    pass_on(flags, value, left)


def climb(height, own, came, sums, flags):
    message = jax.ShapeDtypeStruct((ROWS, W), BF16)
    return pl.pallas_call(
        functools.partial(climb_kernel, height),
        in_specs=[VMEM] * 4,
        out_specs=[VMEM] * 4,
        out_shape=[
            message,
            message,
            jax.ShapeDtypeStruct((3 * RHS, W), BF16),
            jax.ShapeDtypeStruct((sums.shape[0] - RHS, W), F32),
        ],
        compiler_params=PARAMS,
    )(own, came, sums, flags)


def separator(vectors, place, up, above):
    start, distances, index = place
    distance = part(vectors, distances).astype(F32)[index : index + 1]
    known = jnp.zeros((RHS, W), F32)
    for step, value in enumerate(above, 1):
        known = known + jnp.where(distance == float(step), value.astype(F32), 0.0)
    gain = jnp.concatenate([jnp.zeros((SHARE, W), BF16), up[GAIN_B:ROWS]], axis=0)
    return (
        part(vectors, start + 2 * index + 1).astype(F32)
        + times(part(vectors, start + 2 * index), gain)
        - times(above[0], up[:W])
        - times(known.astype(BF16), up[W : 2 * W])
    ).astype(BF16)


def top_kernel(
    vectors, late, came, mine, flags, u3, u4, u3q, u5, u6, u7, near_out, other_out
):
    wide = jnp.concatenate([flag(flags, UPPER - 1)] * 16, axis=0)
    own = jnp.concatenate([mine[:SHARE], mine[GAIN_B:ROWS]], axis=0)
    last = choose(wide, own, came[:W])
    residue = part(late, 7).astype(F32) + came[W:].astype(F32)
    above = [times(residue.astype(BF16), last).astype(BF16)]
    for source, index, up in (
        (late, (0, 6, 2), u7),
        (late, (0, 6, 0), u6),
        (vectors, (14, 16, 0), u5),
        (vectors, (7, 13, 2), u4),
    ):
        above = [separator(source, index, up, above)] + above
    for index, up, out in (((7, 13, 0), u3, near_out), ((7, 13, 1), u3q, other_out)):
        out[:RHS] = separator(vectors, index, up, above)
        for step, value in enumerate(above, 1):
            out[step * RHS : (step + 1) * RHS] = value


def top(vectors, late, came, mine, flags, *ups):
    known = jax.ShapeDtypeStruct(((UPPER - LOW) * RHS, W), BF16)
    return pl.pallas_call(
        top_kernel,
        in_specs=[VMEM] * (5 + len(ups)),
        out_specs=[VMEM] * 2,
        out_shape=[known, known],
        compiler_params=PARAMS,
    )(vectors, late, came, mine, flags, *ups)


def select_known(cases, known):
    for test, ref in cases:

        @pl.when(test)
        def _():
            known[...] = ref[...]


def bottom_kernel(vectors, own, a, b, c, u1, u2, u1q, near_out, other_out, known):
    z = lax.axis_index("col") // 4
    first, last = LEADERS
    select_known(
        [
            ((z == (first ^ k)) | (z == (last ^ k)), ref)
            for k, ref in enumerate((own, a, b, c))
        ],
        known,
    )
    above = [part(known, k) for k in range(UPPER - LOW)]
    above = [separator(vectors, (0, 6, 2), u2, above)] + above
    for index, up, out in (((0, 6, 0), u1, near_out), ((0, 6, 1), u1q, other_out)):
        out[:RHS] = separator(vectors, index, up, above)
        for step, value in enumerate(above, 1):
            out[step * RHS : (step + 1) * RHS] = value


def bottom(vectors, own, a, b, c, u1, u2, u1q):
    known = jax.ShapeDtypeStruct((UPPER * RHS, W), BF16)
    return pl.pallas_call(
        bottom_kernel,
        in_specs=[VMEM] * 8,
        out_specs=[VMEM] * 2,
        out_shape=[known, known],
        scratch_shapes=[pltpu.VMEM(((UPPER - LOW) * RHS, W), BF16)],
        compiler_params=PARAMS,
    )(vectors, own, a, b, c, u1, u2, u1q)


def descend_kernel(uinv, ublk, slots, level, solved, own, a, b, c, out, known):
    place = (lax.axis_index("col") % 4 + 2 * lax.axis_index("gz")) % 4
    select_known(
        [(place == seated, ref) for seated, ref in enumerate((a, own, b, c))], known
    )
    above = [part(known, k) for k in range(UPPER)]
    own_value = jnp.zeros((RHS, W), F32)
    for k, value in enumerate(above):
        own_value = jnp.where(level[...] == float(k + 1), value.astype(F32), own_value)
    out[0, LOCAL_COUNT] = own_value
    for slot in (2, 1, 0):
        distance = part(slots, LOCAL_COUNT + slot)
        distant = jnp.zeros((RHS, W), F32)
        for step, value in enumerate(above, 1):
            distant = distant + jnp.where(distance == float(step), value.astype(F32), 0.0)
        residue = (
            solved[slot]
            - times_rows(above[0], ublk[0, slot, 0])
            - times_rows(distant.astype(BF16), ublk[0, slot, 1])
        )
        value = jnp.where(
            part(slots, slot) > 0.5, times_rows(residue.astype(BF16), uinv[0, slot]), 0.0
        )
        out[0, slot] = value
        if slot == 2:
            above = [value.astype(BF16)] + above


def descend(uinv, ublk, slots, level, solved, own, a, b, c):
    return pl.pallas_call(
        descend_kernel,
        in_specs=[VMEM] * 9,
        out_specs=VMEM,
        out_shape=jax.ShapeDtypeStruct((1, 4, RHS, W), F32),
        scratch_shapes=[pltpu.VMEM((UPPER * RHS, W), BF16)],
        compiler_params=PARAMS,
    )(uinv, ublk, slots, level, solved, own, a, b, c)


def local(rights, linv, uinv, lblk, ublk, widths, far, owner_level):
    first, second, solved, sums, flags, level, slots = begin(
        rights, linv, uinv, lblk, ublk, widths, far, owner_level.reshape(1, DEVICES)
    )
    r2 = send(first, seats(((2, 0), (3, 1))))
    r1 = send(second, seats(((1, 0), (0, 1))))
    r3 = send(second, seats(((3, 0), (2, 1))))
    came = (r1, r2, r3)
    ups_y, message, residues_y, sums = gather(1, first, came, sums, flags)
    came = [send(message, to_leaders(k)) for k in (1, 2, 3)]
    ups_z, message, residues_z, sums = gather(3, message, came, sums, flags)
    came = send(message, across(4 * (LEADERS[0] ^ LEADERS[1])))
    up_5, message, residue_5, sums = climb(5, message, came, sums, flags)
    came = {k: send(message, across(32 * k)) for k in (2, 1, 3)}
    vectors = jnp.concatenate([residues_y, residues_z, residue_5], axis=0)
    vectors = send(vectors, seats(((0, 1),)))
    came = [came[k] for k in (1, 2, 3)]
    ups_x, message, residues_x, sums = gather(6, message, came, sums, flags, False)
    root = sums.astype(BF16)
    across_came = send(jnp.concatenate([message[:W], root], axis=0), layers(0, 1))
    late = jnp.concatenate([residues_x, root], axis=0)
    late = send(late, seats(((0, 1),)))
    known, known_other = top(
        vectors, late, across_came, message, flags, *ups_z, up_5, *ups_x
    )
    a = send(known, from_leaders(1))
    b = send(known_other, from_leaders(2))
    c = send(known_other, from_leaders(3))
    known, known_other = bottom(vectors, known, a, b, c, *ups_y)
    a = send(known, seats(((1, 0),)))
    b = send(known_other, seats(((1, 2),)))
    c = send(known_other, seats(((1, 3),)))
    return descend(uinv, ublk, slots, level, solved, known, a, b, c)


def solution(mesh):
    split = P(AXES)
    in_specs = (split,) * 7 + (P(),)
    return jax.shard_map(local, mesh=mesh, in_specs=in_specs, out_specs=split, check_vma=False)
```
